256 devices in a mesh: layer: 4 (over x), row: 4 (over y), col: 16 (over z, core).
Axes of the slice: x: 4, y: 4, z: 8, core: 2. Of those that a mesh axis runs over, the one named last changes fastest.
Arguments:
- values: bfloat16 [768, 20, 128, 128], P(('row', 'col')), may hold values from -1.1953125 to 1.1953125
- columns: int32 [768, 20], replicated, may hold values from 0 to 767, as said below
- counts: int32 [768], replicated, may hold values from 10 to 20, as said below
Outputs:
- square: bfloat16 [768, 20, 128, 128], P(('row', 'col'), 'layer')
The draws below stay inside these ranges and needn't reach their ends.
Inputs may be any that keep to these rules, and one draw needn't show every extreme that they name: Row i names 20 distinct block columns, each at cyclic distance at most 12 from i modulo 768; only the first counts[i] slots are nonzero blocks. `counts`: some block row has all 20 slots live.
All inputs are finite; a program needn't handle non-finite values.
Results may differ from the reference program's by a relative error of at most 0.001.
Values may be sent and summed in bfloat16 or wider, within the bound.
No kernel may reach another device: no remote copies, remote signals or barrier semaphores. Data moves between devices by JAX's collectives and lax.ppermute only.
A program may use at most 128 MiB of HBM per device.

```python
import jax
import jax.numpy as jnp
from jax import lax

B = 128
K = 20
BAND = 12
NB = 768


def draw_columns(key, part):
    width = 2 * BAND + 1
    scores = jax.random.randint(key, (NB, width), 0, 1 << 20) * width + jnp.arange(width, dtype=jnp.int32)[None, :]
    order = jnp.argsort(scores, axis=1).astype(jnp.int32)
    offsets = order[:, :K] - BAND
    return ((jnp.arange(NB, dtype=jnp.int32)[:, None] + offsets) % NB).astype(jnp.int32)


def draw_counts(key, part):
    drawn = jax.random.randint(key, (NB,), K // 2, K + 1)
    return drawn.at[0].set(K).astype(jnp.int32)


def block_levels(own_key, shape, shards, smallest, largest):
    def one(dim, blocks):
        draws = jax.random.uniform(jax.random.fold_in(jax.random.fold_in(own_key, 6), dim), (blocks,), jnp.float32, smallest / len(shards), largest / len(shards))
        return jnp.repeat(jnp.exp(draws), shape[dim] // blocks).reshape((-1,) + (1,) * (len(shape) - dim - 1))

    factor_of = one(*shards[0])
    for cut in shards[1:]:
        factor_of = factor_of * one(*cut)
    return factor_of


def gaussian(own_key, shape, scale, reach, split=(), kind=jnp.bfloat16):
    array = jax.random.normal(own_key, shape, jnp.float32) * scale
    if len(split) > 0:
        array = block_levels(own_key, shape, split, -0.22, 0.18) * array
    return jnp.clip(array, min=-reach, max=reach).astype(kind)


def setup_inputs(seed: int = 0) -> dict:
    splits = jax.random.split(jax.random.key(seed), 4)
    return {
        "values": gaussian(splits[0], (NB, K, B, B), 0.2, 1.1953125, ((0, 64),)),
        "columns": draw_columns(jax.random.fold_in(splits[3], 71), 0),
        "counts": draw_counts(jax.random.fold_in(splits[3], 71), 0),
    }


def reference(values, columns, counts):
    slot_ids = jnp.arange(K).astype(jnp.int32)
    live_mask = slot_ids[None, :] < counts[:, None]

    def one_row(row_index):
        cols_row = columns[row_index]
        live_row = live_mask[row_index]
        cols_far = jnp.take(columns, cols_row, axis=0)
        live_far = jnp.take(live_mask, cols_row, axis=0) & live_row[:, None]
        match = (cols_far[None, :, :] == cols_row[:, None, None]) & live_far[None, :, :] & live_row[:, None, None]
        found = jnp.any(match, axis=2)
        which = jnp.sum(jnp.where(match, slot_ids[None, None, :], 0), axis=2).astype(jnp.int32)
        picked = values[cols_row[None, :], which]
        picked = jnp.where(found[:, :, None, None], picked.astype(jnp.float32), jnp.float32(0.0))
        a_row = values[row_index].astype(jnp.float32)
        total = jnp.einsum("mab,pmbc->pac", a_row, picked)
        return total.astype(jnp.bfloat16)

    return lax.map(one_row, jnp.arange(NB).astype(jnp.int32))
```

```python
import functools

import jax
import jax.numpy as jnp
from jax import lax
from jax.experimental import pallas as pl
from jax.experimental.pallas import tpu as pltpu
from jax.sharding import PartitionSpec as P

BAND = 12
STRIDE = 64
UNROLL = 4
FIRST = 104
ANY = pl.BlockSpec(memory_space=pl.ANY)
SMEM = pl.BlockSpec(memory_space=pltpu.SMEM)
VMEM = pl.BlockSpec(memory_space=pltpu.VMEM)


def pack_kernel(start, size, idx_ref, blocks_ref, out_ref, held, read_sem, write_sem):
    group = 8

    def read(g, carry):
        for u in range(group):
            p = g * group + u
            pltpu.make_async_copy(
                blocks_ref.at[idx_ref[start + p]], held.at[p], read_sem.at[g]
            ).start()
        return carry

    lax.fori_loop(0, size // group, read, 0)

    def write(g, carry):
        part = pl.ds(g * group, group)
        pltpu.make_async_copy(
            blocks_ref.at[pl.ds(0, group)], held.at[part], read_sem.at[g]
        ).wait()
        pltpu.make_async_copy(held.at[part], out_ref.at[part], write_sem).start()
        return carry

    lax.fori_loop(0, size // group, write, 0)
    pltpu.make_async_copy(held, out_ref, write_sem).wait()


def pack(idx, blocks, start, size):
    shape = (size,) + blocks.shape[1:]
    return pl.pallas_call(
        functools.partial(pack_kernel, start, size),
        out_shape=jax.ShapeDtypeStruct(shape, blocks.dtype),
        in_specs=[SMEM, ANY],
        out_specs=ANY,
        scratch_shapes=[
            pltpu.VMEM(shape, blocks.dtype),
            pltpu.SemaphoreType.DMA((size // 8,)),
            pltpu.SemaphoreType.DMA,
        ],
        compiler_params=pltpu.CompilerParams(vmem_limit_bytes=8 << 20),
        name="pack",
    )(idx, blocks)


def run_list(entries, length, a_ref, v_ref, acc_ref):
    def step(t, carry):
        parts = []
        for u in range(UNROLL):
            e0 = entries[(t * UNROLL + u) * 2]
            e1 = entries[(t * UNROLL + u) * 2 + 1]
            lhs = jnp.concatenate(
                [a_ref[(e0 >> 10) & 255], a_ref[(e1 >> 10) & 255]], axis=1
            )
            rhs = jnp.concatenate([v_ref[e0 & 1023], v_ref[e1 & 1023]], axis=0)
            parts.append(
                (e0 >> 18, jnp.dot(lhs, rhs, preferred_element_type=jnp.float32))
            )
        for out, part in parts:
            acc_ref[out] += part
        return carry

    lax.fori_loop(0, length // (2 * UNROLL), step, 0)


def local_kernel(
    rows,
    slots,
    quarter,
    first,
    params_ref,
    table_ref,
    place_ref,
    blocks_ref,
    inner_ref,
    acc_ref,
    near_ref,
    extra_ref,
    sizes_ref,
    own_ref,
    v_ref,
    sem,
):
    count = rows * slots
    zero_at = 2 * count
    outs = rows * quarter
    loads = [
        pltpu.make_async_copy(ref, v_ref.at[pl.ds(at, count)], sem.at[n])
        for n, (ref, at) in enumerate(((blocks_ref, 0), (inner_ref, count)))
    ]
    for load in loads:
        load.start()
    v_ref[zero_at] = jnp.zeros(v_ref.shape[1:], v_ref.dtype)

    def clear(o, carry):
        acc_ref[o] = jnp.zeros(acc_ref.shape[1:], acc_ref.dtype)
        return carry

    lax.fori_loop(0, outs + 1, clear, 0)
    start_slot = params_ref[0]

    def one_output(o, ends):
        i = o // quarter
        p = start_slot + o % quarter
        j_at = place_ref[i * slots + p]
        alive = j_at < 3 * rows

        def terms(ends):
            e_own, e_near, e_extra = ends
            for m in range(slots):
                k_at = place_ref[i * slots + m]
                b = table_ref[k_at * STRIDE + j_at - k_at + 2 * BAND]
                tag = (o << 18) | ((i * slots + m) << 10)
                kind = b >> 10
                entry = tag | (b & 1023)
                own_ref[e_own] = entry
                near_ref[e_near] = entry
                extra_ref[e_extra] = entry
                e_own += jnp.where(kind == 1, 1, 0)
                e_near += jnp.where(kind == 2, 1, 0)
                e_extra += jnp.where(kind == 3, 1, 0)
            tag = (o << 18) | ((i * slots) << 10)
            own_ref[e_own] = tag | zero_at
            near_ref[e_near] = tag | first
            extra_ref[e_extra] = tag | (BOUND - first)
            return (
                e_own + (e_own & 1),
                e_near + (e_near & 1),
                e_extra + (e_extra & 1),
            )

        return lax.cond(alive, terms, lambda ends: ends, ends)

    zero = jnp.int32(0)
    e_own, e_near, e_extra = lax.fori_loop(0, outs, one_output, (zero, zero, zero))
    for u in range(2 * UNROLL):
        own_ref[e_own + u] = (outs << 18) | zero_at
        near_ref[e_near + u] = (outs << 18) | first
        extra_ref[e_extra + u] = (outs << 18) | (BOUND - first)
    size = 2 * UNROLL
    sizes_ref[0] = (e_near + size - 1) // size * size
    sizes_ref[1] = (e_extra + size - 1) // size * size
    for load in loads:
        load.wait()
    run_list(own_ref, (e_own + size - 1) // size * size, v_ref, v_ref, acc_ref)


BOUND = 200


def local_products(params, table, place, blocks, inner, rows, slots, quarter):
    edge = blocks.shape[-1]
    outs = rows * quarter
    length = outs * slots + 4 * UNROLL
    int_list = jax.ShapeDtypeStruct((length,), jnp.int32)
    return pl.pallas_call(
        functools.partial(local_kernel, rows, slots, quarter, FIRST),
        out_shape=(
            jax.ShapeDtypeStruct((outs + 1, edge, edge), jnp.float32),
            int_list,
            int_list,
            jax.ShapeDtypeStruct((8,), jnp.int32),
        ),
        in_specs=[SMEM, SMEM, SMEM, ANY, ANY],
        out_specs=(VMEM, SMEM, SMEM, SMEM),
        scratch_shapes=[
            pltpu.SMEM((length,), jnp.int32),
            pltpu.VMEM((2 * rows * slots + 1, edge, edge), blocks.dtype),
            pltpu.SemaphoreType.DMA((2,)),
        ],
        compiler_params=pltpu.CompilerParams(vmem_limit_bytes=26 << 20),
        cost_estimate=pl.CostEstimate(
            flops=10 * 10**9, bytes_accessed=24 * 10**6, transcendentals=0
        ),
        name="local_products",
    )(params, table, place, blocks, inner)


def remote_kernel(chunks, outs, *refs):
    sizes_ref = refs[0]
    lists = refs[1 : 1 + chunks]
    acc_in, blocks_ref = refs[1 + chunks : 3 + chunks]
    halos = refs[3 + chunks : 3 + 2 * chunks]
    out_ref = refs[3 + 2 * chunks]
    a_ref, acc_ref = refs[4 + 2 * chunks : 6 + 2 * chunks]
    stores = refs[6 + 2 * chunks : 6 + 3 * chunks]
    sem = refs[6 + 3 * chunks]
    pairs = [(acc_in, acc_ref), (blocks_ref, a_ref)]
    for halo, store in zip(halos, stores):
        pairs.append((halo, store.at[pl.ds(0, halo.shape[0])]))
    copies = [
        pltpu.make_async_copy(source, target, sem.at[n])
        for n, (source, target) in enumerate(pairs)
    ]
    for copy in copies:
        copy.start()
    for halo, store in zip(halos, stores):
        store[halo.shape[0]] = jnp.zeros(store.shape[1:], store.dtype)
    for copy in copies:
        copy.wait()
    for c in range(chunks):
        run_list(lists[c], sizes_ref[c], a_ref, stores[c], acc_ref)

    def finish(o, carry):
        out_ref[o] = acc_ref[o].astype(out_ref.dtype)
        return carry

    lax.fori_loop(0, outs, finish, 0, unroll=2)


def remote_products(sizes, lists, acc, blocks, halos, outs):
    chunks = len(lists)
    edge = blocks.shape[-1]
    return pl.pallas_call(
        functools.partial(remote_kernel, chunks, outs),
        out_shape=jax.ShapeDtypeStruct((outs, edge, edge), blocks.dtype),
        in_specs=[SMEM] * (1 + chunks) + [ANY] * (2 + chunks),
        out_specs=VMEM,
        scratch_shapes=[
            pltpu.VMEM(blocks.shape, blocks.dtype),
            pltpu.VMEM((outs + 1, edge, edge), jnp.float32),
        ]
        + [
            pltpu.VMEM((halo.shape[0] + 1, edge, edge), blocks.dtype) for halo in halos
        ]
        + [pltpu.SemaphoreType.DMA((2 + chunks,))],
        compiler_params=pltpu.CompilerParams(vmem_limit_bytes=26 << 20),
        name="remote_products",
    )(sizes, *lists, acc, blocks, *halos)


def or_reduce(x, axis):
    return lax.reduce(x, jnp.uint32(0), lax.bitwise_or, (axis,))


def bit_masks(off, live):
    bits = jnp.where(live, jnp.uint32(1) << off.astype(jnp.uint32), jnp.uint32(0))
    return or_reduce(bits, 1), bits


def needed(k_mask, i_mask, i_part, later):
    rows = k_mask.shape[-1]
    kk = lax.broadcasted_iota(jnp.int32, (rows, rows), 0)
    ii = lax.broadcasted_iota(jnp.int32, (rows, rows), 1)
    ahead = ii - kk if later else kk - ii
    valid = ahead <= 0
    shift = jnp.where(valid, rows + ahead, 0).astype(jnp.uint32)
    at = BAND - shift if later else BAND + shift
    has = valid & (((i_mask[..., None, :] >> at) & 1) == 1)
    moved = i_part[..., None, :] << shift if later else i_part[..., None, :] >> shift
    return k_mask & or_reduce(jnp.where(has, moved, jnp.uint32(0)), moved.ndim - 1)


def most_needed(columns, counts, layers):
    total_rows, slots = columns.shape
    quarter = slots // layers
    rows_id = jnp.arange(total_rows, dtype=jnp.int32)
    off = (columns - rows_id[:, None] + BAND) % total_rows
    slot_ids = jnp.arange(slots, dtype=jnp.int32)
    live = slot_ids[None, :] < counts[:, None]
    mask, bits = bit_masks(off, live)
    part = jnp.stack(
        [or_reduce(bits[:, q * quarter : (q + 1) * quarter], 1) for q in range(layers)]
    )
    mask_wrap = jnp.concatenate([mask[-BAND:], mask, mask[:BAND]])
    part_wrap = jnp.concatenate([part[:, -BAND:], part, part[:, :BAND]], axis=1)
    kk = rows_id % BAND
    up = jnp.zeros_like(part)
    down = jnp.zeros_like(part)
    for s in range(1, BAND + 1):
        i_mask = mask_wrap[BAND + s : BAND + s + total_rows]
        i_part = part_wrap[:, BAND + s : BAND + s + total_rows]
        has = (((i_mask >> (BAND - s)) & 1) == 1) & (kk + s >= BAND)
        up = up | jnp.where(has, i_part << s, jnp.uint32(0))
        i_mask = mask_wrap[BAND - s : BAND - s + total_rows]
        i_part = part_wrap[:, BAND - s : BAND - s + total_rows]
        has = (((i_mask >> (BAND + s)) & 1) == 1) & (kk - s < 0)
        down = down | jnp.where(has, i_part >> s, jnp.uint32(0))
    odd = (rows_id // BAND) % 2 == 1
    asked = jnp.where(odd, up, down) & mask
    per_row = lax.population_count(asked).astype(jnp.int32)
    return jnp.max(jnp.sum(per_row.reshape(layers, -1, BAND), axis=2))


def per_device(values, columns, counts):
    rows, slots, edge, _ = values.shape
    layers = lax.axis_size("layer")
    quarter = slots // layers
    start_slot = lax.axis_index("layer") * quarter
    total_rows = columns.shape[0]
    group = lax.axis_index(("row", "col"))
    groups = lax.axis_size(("row", "col"))
    even = group % 2 == 0
    first_row = group * rows
    blocks = values.reshape((-1, edge, edge))
    span = rows * slots

    inner = lax.ppermute(blocks, ("row", "col"), [(g, g ^ 1) for g in range(groups)])

    all_cols = jnp.concatenate([columns[-rows:], columns, columns[:rows]], axis=0)
    all_counts = jnp.concatenate([counts[-rows:], counts, counts[:rows]], axis=0)
    cols = lax.dynamic_slice_in_dim(all_cols, first_row, 3 * rows, 0)
    cnts = lax.dynamic_slice_in_dim(all_counts, first_row, 3 * rows, 0)
    row_ids = first_row - rows + jnp.arange(3 * rows, dtype=jnp.int32)
    off = (cols - row_ids[:, None] + BAND) % total_rows
    slot_ids = jnp.arange(slots, dtype=jnp.int32)[None, :]
    live = slot_ids < cnts[:, None]
    mask, bits = bit_masks(off, live)
    mine = (slot_ids >= start_slot) & (slot_ids < start_slot + quarter)
    part = or_reduce(jnp.where(mine, bits, jnp.uint32(0)), 1)
    mask = mask.reshape(3, rows)
    part = part.reshape(3, rows)
    off = off.reshape(3, rows, slots)
    live = live.reshape(3, rows, slots)

    def pair(x):
        return jnp.where(even, x[:2], x[1:])

    mask2, part2, off2, live2 = pair(mask), pair(part), pair(off), pair(live)
    ask = jnp.stack(
        [
            needed(mask2[0], mask2[1], part2[1], True),
            needed(mask2[1], mask2[0], part2[0], False),
        ]
    )
    need = (((ask[:, :, None] >> off2.astype(jnp.uint32)) & 1) == 1) & live2
    need = jnp.stack([need[0, ::-1], need[1]]).reshape(2, span)
    before = (
        lax.broadcasted_iota(jnp.int32, (span, span), 0)
        < lax.broadcasted_iota(jnp.int32, (span, span), 1)
    ).astype(jnp.bfloat16)
    pos = jnp.dot(
        need.astype(jnp.bfloat16), before, preferred_element_type=jnp.float32
    ).astype(jnp.int32)
    ids = jnp.arange(span, dtype=jnp.int32)
    ids_up = (rows - 1 - ids // slots) * slots + ids % slots
    give, give_pos = jnp.where(even, need[1], need[0]), jnp.where(even, pos[1], pos[0])
    give_ids = jnp.where(even, ids, ids_up)
    get, get_pos = jnp.where(even, need[0], need[1]), jnp.where(even, pos[0], pos[1])
    hit = give[:, None] & (
        give_pos[:, None] == jnp.arange(BOUND, dtype=jnp.int32)[None, :]
    )
    send_idx = jnp.sum(jnp.where(hit, give_ids[:, None], 0), axis=0)

    outer_pairs = [
        (g, (g - 1) % groups if g % 2 == 0 else (g + 1) % groups) for g in range(groups)
    ]
    outer = lax.ppermute(pack(send_idx, blocks, 0, FIRST), ("row", "col"), outer_pairs)

    code = jnp.where(get_pos < FIRST, (2 << 10) + get_pos, (3 << 10) + get_pos - FIRST)
    code = jnp.where(get, code, 0).reshape(rows, slots)
    code = jnp.where(even, code[::-1], code)
    ids = ids.reshape(rows, slots)
    own = jnp.where(live[1], (1 << 10) + ids, 0)
    near = jnp.where(even, live[2], live[0])
    near = jnp.where(near, (1 << 10) + span + ids, 0)
    codes = jnp.concatenate(
        [jnp.where(even, code, near), own, jnp.where(even, near, code)], axis=0
    )
    off3 = off.reshape(3 * rows, slots)
    at = lax.broadcasted_iota(jnp.int32, (1, 1, STRIDE), 2)
    table = jnp.sum(
        jnp.where(off3[:, :, None] + BAND == at, codes[:, :, None], 0), axis=1
    ).reshape(-1)
    table = jnp.concatenate([table, jnp.zeros((STRIDE,), jnp.int32)])
    place = jnp.where(
        live[1], jnp.arange(rows, dtype=jnp.int32)[:, None] + off[1], 3 * rows
    ).reshape(-1)
    params = jnp.full((8,), start_slot, jnp.int32)

    acc, near, extra, sizes = local_products(
        params, table, place, blocks, inner, rows, slots, quarter
    )
    outs = rows * quarter
    more = most_needed(columns, counts, layers) > FIRST

    def with_extra():
        late = pack(send_idx, blocks, FIRST, BOUND - FIRST)
        late = lax.ppermute(late, ("row", "col"), outer_pairs)
        return remote_products(sizes, [near, extra], acc, blocks, [outer, late], outs)

    def without():
        return remote_products(sizes, [near], acc, blocks, [outer], outs)

    square = lax.cond(more, with_extra, without)
    return square.reshape(rows, quarter, edge, edge)


def solution(mesh):
    return jax.shard_map(
        per_device,
        mesh=mesh,
        in_specs=(P(("row", "col"), None, None, None), P(), P()),
        out_specs=P(("row", "col"), "layer", None, None),
        check_vma=False,
    )
```

```python
import functools

import jax
import jax.numpy as jnp
from jax import lax
from jax.experimental import pallas as pl
from jax.experimental.pallas import tpu as pltpu
from jax.sharding import PartitionSpec as P

BAND = 12
STRIDE = 64
WIDE = 16
UNROLL = 4
NEAR_ROWS = 6
NEAR_SLOTS = 12
FIRST = 60
BOUND = 132
ANY = pl.BlockSpec(memory_space=pl.ANY)
SMEM = pl.BlockSpec(memory_space=pltpu.SMEM)
VMEM = pl.BlockSpec(memory_space=pltpu.VMEM)


def pack_kernel(start, size, idx_ref, blocks_ref, out_ref, held, read_sem, write_sem):
    group = 4

    def read(g, carry):
        for u in range(group):
            p = g * group + u
            pltpu.make_async_copy(
                blocks_ref.at[idx_ref[start + p]], held.at[p], read_sem.at[g]
            ).start()
        return carry

    lax.fori_loop(0, size // group, read, 0)

    def write(g, carry):
        part = pl.ds(g * group, group)
        pltpu.make_async_copy(
            blocks_ref.at[pl.ds(0, group)], held.at[part], read_sem.at[g]
        ).wait()
        pltpu.make_async_copy(held.at[part], out_ref.at[part], write_sem).start()
        return carry

    lax.fori_loop(0, size // group, write, 0)
    pltpu.make_async_copy(held, out_ref, write_sem).wait()


def pack(idx, blocks, start, size):
    shape = (size,) + blocks.shape[1:]
    return pl.pallas_call(
        functools.partial(pack_kernel, start, size),
        out_shape=jax.ShapeDtypeStruct(shape, blocks.dtype),
        in_specs=[SMEM, ANY],
        out_specs=ANY,
        scratch_shapes=[
            pltpu.VMEM(shape, blocks.dtype),
            pltpu.SemaphoreType.DMA((size // 4,)),
            pltpu.SemaphoreType.DMA,
        ],
        compiler_params=pltpu.CompilerParams(vmem_limit_bytes=8 << 20),
        name="pack",
    )(idx, blocks)


def run_list(entries, length, a_ref, v_ref, acc_ref):
    def steps(begin, count, carry):
        parts = []
        for u in range(count):
            e0 = entries[(begin + u) * 2]
            e1 = entries[(begin + u) * 2 + 1]
            lhs = jnp.concatenate(
                [a_ref[(e0 >> 10) & 255], a_ref[(e1 >> 10) & 255]], axis=1
            )
            rhs = jnp.concatenate([v_ref[e0 & 1023], v_ref[e1 & 1023]], axis=0)
            parts.append(
                (e0 >> 18, jnp.dot(lhs, rhs, preferred_element_type=jnp.float32))
            )
        for out, part in parts:
            acc_ref[out] += part
        return carry

    pairs = length // 2
    wide = pairs // WIDE
    lax.fori_loop(0, wide, lambda t, c: steps(t * WIDE, WIDE, c), 0)
    rest = (pairs - wide * WIDE) // UNROLL
    lax.fori_loop(0, rest, lambda t, c: steps(wide * WIDE + t * UNROLL, UNROLL, c), 0)


def local_kernel(
    rows,
    slots,
    quarter,
    start_ref,
    table_ref,
    place_ref,
    blocks_ref,
    inner_ref,
    acc_ref,
    far_ref,
    size_ref,
    own_ref,
    inner_v,
    sem,
):
    count = rows * slots
    outs = rows * quarter
    size = 2 * UNROLL
    load = pltpu.make_async_copy(inner_ref, inner_v.at[pl.ds(1 + count, count)], sem.at[0])
    load.start()
    load_own = pltpu.make_async_copy(blocks_ref, inner_v.at[pl.ds(1, count)], sem.at[1])
    load_own.start()
    inner_v[0] = jnp.zeros(inner_v.shape[1:], inner_v.dtype)

    def clear(o, carry):
        acc_ref[o] = jnp.zeros(acc_ref.shape[1:], acc_ref.dtype)
        return carry

    lax.fori_loop(0, outs + 1, clear, 0)
    start_slot = start_ref[0]

    def one_row(i, ends):
        base = i * slots
        row_tag = base << 10
        terms_at = [place_ref[base + m] * (STRIDE - 1) for m in range(slots)]

        def one_output(p, ends):
            j_at = place_ref[base + start_slot + p]
            tag = row_tag + ((i * quarter + p) << 18)

            def terms(ends):
                e_own, e_far = ends
                for m in range(slots):
                    code = table_ref[terms_at[m] + (j_at + 2 * BAND)]
                    entry = (code & 1023) + (tag + (m << 10))
                    own_ref[e_own] = entry
                    far_ref[e_far] = entry
                    e_own += (code >> 10) & 1
                    e_far += code >> 11
                own_ref[e_own] = tag
                far_ref[e_far] = tag
                return e_own + (e_own & 1), e_far + (e_far & 1)

            return lax.cond(j_at < 3 * rows, terms, lambda ends: ends, ends)

        return lax.fori_loop(0, quarter, one_output, ends)

    zero = jnp.int32(0)
    e_own, e_far = lax.fori_loop(0, rows, one_row, (zero, zero))
    for u in range(size):
        own_ref[e_own + u] = outs << 18
        far_ref[e_far + u] = outs << 18
    size_ref[0] = (e_far + size - 1) // size * size
    load_own.wait()
    load.wait()
    run_list(own_ref, (e_own + size - 1) // size * size, inner_v.at[pl.ds(1, count)], inner_v, acc_ref)


def local_products(start, table, place, blocks, inner, rows, slots, quarter):
    edge = blocks.shape[-1]
    outs = rows * quarter
    length = outs * slots + 4 * UNROLL
    return pl.pallas_call(
        functools.partial(local_kernel, rows, slots, quarter),
        out_shape=(
            jax.ShapeDtypeStruct((outs + 1, edge, edge), jnp.float32),
            jax.ShapeDtypeStruct((length,), jnp.int32),
            jax.ShapeDtypeStruct((8,), jnp.int32),
        ),
        in_specs=[SMEM, SMEM, SMEM, ANY, ANY],
        out_specs=(VMEM, SMEM, SMEM),
        scratch_shapes=[
            pltpu.SMEM((length,), jnp.int32),
            pltpu.VMEM((2 * rows * slots + 1, edge, edge), blocks.dtype),
            pltpu.SemaphoreType.DMA((2,)),
        ],
        compiler_params=pltpu.CompilerParams(vmem_limit_bytes=26 << 20),
        cost_estimate=pl.CostEstimate(
            flops=10 * 10**9, bytes_accessed=24 * 10**6, transcendentals=0
        ),
        name="local_products",
    )(start, table, place, blocks, inner)


def far_kernel(
    rows,
    quarter,
    more_ref,
    size_ref,
    list_ref,
    acc_in,
    blocks_ref,
    near0_ref,
    near1_ref,
    near2_ref,
    near3_ref,
    first_ref,
    late_ref,
    out_ref,
    a_ref,
    acc_ref,
    v_ref,
    held,
    sem,
):
    nears = (near0_ref, near1_ref, near2_ref, near3_ref)
    near, first, late = near0_ref.shape[0], first_ref.shape[0], late_ref.shape[0]
    at = 1 + len(nears) * near
    late_copy = pltpu.make_async_copy(
        late_ref, v_ref.at[pl.ds(at + first, late)], sem.at[3]
    )
    pairs = [(first_ref, v_ref.at[pl.ds(at, first)]), (acc_in, acc_ref), (blocks_ref, a_ref)]
    copies = [
        pltpu.make_async_copy(source, target, sem.at[n])
        for n, (source, target) in enumerate(pairs)
    ]
    me = more_ref[1]
    for away, ref in enumerate(nears):
        source = lax.rem(me + len(nears) - away, len(nears))
        copies.append(
            pltpu.make_async_copy(
                ref, v_ref.at[pl.ds(1 + source * near, near)], sem.at[5 + away]
            )
        )
    for copy in copies:
        copy.start()
    v_ref[0] = jnp.zeros(v_ref.shape[1:], v_ref.dtype)

    @pl.when(more_ref[0] > 0)
    def _():
        late_copy.start()
        late_copy.wait()

    for copy in copies:
        copy.wait()
    run_list(list_ref, size_ref[0], a_ref, v_ref, acc_ref)

    def finish(i, carry):
        part = pl.ds(i * quarter, quarter)
        held[part] = acc_ref[part].astype(held.dtype)
        pltpu.make_async_copy(held.at[part], out_ref.at[part], sem.at[4]).start()
        return carry

    lax.fori_loop(0, rows, finish, 0)
    pltpu.make_async_copy(held, out_ref, sem.at[4]).wait()


def far_products(flags, size, entries, acc, blocks, nears, first, late, rows, quarter):
    edge = blocks.shape[-1]
    outs = rows * quarter
    held = 1 + len(nears) * nears[0].shape[0] + first.shape[0] + late.shape[0]
    return pl.pallas_call(
        functools.partial(far_kernel, rows, quarter),
        out_shape=jax.ShapeDtypeStruct((outs, edge, edge), blocks.dtype),
        in_specs=[SMEM] * 3 + [ANY] * (4 + len(nears)),
        out_specs=ANY,
        scratch_shapes=[
            pltpu.VMEM(blocks.shape, blocks.dtype),
            pltpu.VMEM((outs + 1, edge, edge), jnp.float32),
            pltpu.VMEM((held, edge, edge), blocks.dtype),
            pltpu.VMEM((outs, edge, edge), blocks.dtype),
            pltpu.SemaphoreType.DMA((5 + len(nears),)),
        ],
        compiler_params=pltpu.CompilerParams(vmem_limit_bytes=26 << 20),
        name="far_products",
    )(flags, size, entries, acc, blocks, *nears, first, late)


def blank(shape, dtype):
    return pl.pallas_call(
        lambda out_ref: None,
        out_shape=jax.ShapeDtypeStruct(shape, dtype),
        out_specs=ANY,
        name="blank",
    )()


def or_reduce(x, axis):
    return lax.reduce(x, jnp.uint32(0), lax.bitwise_or, (axis,))


def bit_masks(off, live):
    bits = jnp.where(live, jnp.uint32(1) << off.astype(jnp.uint32), jnp.uint32(0))
    return or_reduce(bits, 1), bits


def needed(k_mask, i_mask, i_part, later):
    rows = k_mask.shape[-1]
    kk = lax.broadcasted_iota(jnp.int32, (rows, rows), 0)
    ii = lax.broadcasted_iota(jnp.int32, (rows, rows), 1)
    ahead = ii - kk if later else kk - ii
    valid = ahead <= 0
    shift = jnp.where(valid, rows + ahead, 0).astype(jnp.uint32)
    at = BAND - shift if later else BAND + shift
    has = valid & (((i_mask[..., None, :] >> at) & 1) == 1)
    moved = i_part[..., None, :] << shift if later else i_part[..., None, :] >> shift
    return k_mask & or_reduce(jnp.where(has, moved, jnp.uint32(0)), moved.ndim - 1)


def most_needed(columns, counts, layers):
    total_rows, slots = columns.shape
    quarter = slots // layers
    rows_id = jnp.arange(total_rows, dtype=jnp.int32)
    off = (columns - rows_id[:, None] + BAND) % total_rows
    slot_ids = jnp.arange(slots, dtype=jnp.int32)
    live = slot_ids[None, :] < counts[:, None]
    mask, bits = bit_masks(off, live)
    part = jnp.stack(
        [or_reduce(bits[:, q * quarter : (q + 1) * quarter], 1) for q in range(layers)]
    )
    mask_wrap = jnp.concatenate([mask[-BAND:], mask, mask[:BAND]])
    part_wrap = jnp.concatenate([part[:, -BAND:], part, part[:, :BAND]], axis=1)
    kk = rows_id % BAND
    up = jnp.zeros_like(part)
    down = jnp.zeros_like(part)
    for s in range(1, BAND + 1):
        i_mask = mask_wrap[BAND + s : BAND + s + total_rows]
        i_part = part_wrap[:, BAND + s : BAND + s + total_rows]
        has = (((i_mask >> (BAND - s)) & 1) == 1) & (kk + s >= BAND)
        up = up | jnp.where(has, i_part << s, jnp.uint32(0))
        i_mask = mask_wrap[BAND - s : BAND - s + total_rows]
        i_part = part_wrap[:, BAND - s : BAND - s + total_rows]
        has = (((i_mask >> (BAND + s)) & 1) == 1) & (kk - s < 0)
        down = down | jnp.where(has, i_part >> s, jnp.uint32(0))
    odd = (rows_id // BAND) % 2 == 1
    fixed = or_reduce(bits[:, :NEAR_SLOTS], 1)
    close = jnp.where(odd, kk >= BAND - NEAR_ROWS, kk < NEAR_ROWS)
    asked = jnp.where(odd, up, down) & mask & jnp.where(close, ~fixed, ~jnp.uint32(0))
    per_row = lax.population_count(asked).astype(jnp.bfloat16)
    member = rows_id[:, None] // BAND == jnp.arange(total_rows // BAND)[None, :]
    per_group = jnp.dot(
        per_row, member.astype(jnp.bfloat16), preferred_element_type=jnp.float32
    )
    return jnp.max(per_group)


def per_device(values, columns, counts):
    rows, slots, edge, _ = values.shape
    layers = lax.axis_size("layer")
    quarter = slots // layers
    start_slot = lax.axis_index("layer") * quarter
    total_rows = columns.shape[0]
    group = lax.axis_index(("row", "col"))
    groups = lax.axis_size(("row", "col"))
    even = group % 2 == 0
    first_row = group * rows
    blocks = values.reshape((-1, edge, edge))
    span = rows * slots

    inner = lax.ppermute(blocks, ("row", "col"), [(g, g ^ 1) for g in range(groups)])

    share = NEAR_SLOTS // layers
    layer = lax.axis_index("layer")
    outer_pairs = [
        (g, (g - 1) % groups if g % 2 == 0 else (g + 1) % groups) for g in range(groups)
    ]
    near_rows = lax.dynamic_slice(
        values,
        (jnp.where(even, 0, rows - NEAR_ROWS), layer * share, 0, 0),
        (NEAR_ROWS, share, edge, edge),
    ).reshape(-1, edge, edge)
    near_mine = lax.ppermute(near_rows, ("row", "col"), outer_pairs)
    all_cols = jnp.concatenate([columns[-rows:], columns, columns[:rows]], axis=0)
    all_counts = jnp.concatenate([counts[-rows:], counts, counts[:rows]], axis=0)
    cols = lax.dynamic_slice_in_dim(all_cols, first_row, 3 * rows, 0)
    cnts = lax.dynamic_slice_in_dim(all_counts, first_row, 3 * rows, 0)
    row_ids = first_row - rows + jnp.arange(3 * rows, dtype=jnp.int32)
    off = (cols - row_ids[:, None] + BAND) % total_rows
    slot_ids = jnp.arange(slots, dtype=jnp.int32)[None, :]
    live = slot_ids < cnts[:, None]
    mask, bits = bit_masks(off, live)
    mine = (slot_ids >= start_slot) & (slot_ids < start_slot + quarter)
    part = or_reduce(jnp.where(mine, bits, jnp.uint32(0)), 1)
    mask = mask.reshape(3, rows)
    part = part.reshape(3, rows)
    off = off.reshape(3, rows, slots)
    live = live.reshape(3, rows, slots)

    def pair(x):
        return jnp.where(even, x[:2], x[1:])

    mask2, part2, off2, live2 = pair(mask), pair(part), pair(off), pair(live)
    ask = jnp.stack(
        [
            needed(mask2[0], mask2[1], part2[1], True),
            needed(mask2[1], mask2[0], part2[0], False),
        ]
    )
    need = (((ask[:, :, None] >> off2.astype(jnp.uint32)) & 1) == 1) & live2
    fixed = (jnp.arange(rows)[:, None] < NEAR_ROWS) & (slot_ids < NEAR_SLOTS)
    need = jnp.stack([need[0, ::-1], need[1]]) & ~fixed
    need = need.reshape(2, span)
    before = (
        lax.broadcasted_iota(jnp.int32, (span, span), 0)
        < lax.broadcasted_iota(jnp.int32, (span, span), 1)
    ).astype(jnp.bfloat16)
    pos = jnp.dot(
        need.astype(jnp.bfloat16), before, preferred_element_type=jnp.float32
    ).astype(jnp.int32)
    ids = jnp.arange(span, dtype=jnp.int32)
    ids_up = (rows - 1 - ids // slots) * slots + ids % slots
    give, give_pos = jnp.where(even, need[1], need[0]), jnp.where(even, pos[1], pos[0])
    give_ids = jnp.where(even, ids, ids_up)
    get, get_pos = jnp.where(even, need[0], need[1]), jnp.where(even, pos[0], pos[1])
    hit = give[:, None] & (
        give_pos[:, None] == jnp.arange(BOUND, dtype=jnp.int32)[None, :]
    )
    send_idx = jnp.sum(jnp.where(hit, give_ids[:, None], 0), axis=0)

    columns, counts, send_idx, near_mine = lax.optimization_barrier(
        (columns, counts, send_idx, near_mine)
    )
    nears = [near_mine] + [
        lax.ppermute(near_mine, "layer", [(x, (x + d) % layers) for x in range(layers)])
        for d in range(1, layers)
    ]
    packed = pack(send_idx, blocks, 0, FIRST)
    outer = lax.ppermute(packed, ("row", "col"), outer_pairs)

    code = jnp.where(get, (2 << 10) + 1 + NEAR_ROWS * NEAR_SLOTS + get_pos, 0)
    code = jnp.where(even, code.reshape(rows, slots)[::-1], code.reshape(rows, slots))
    row_at = jnp.arange(rows, dtype=jnp.int32)[:, None] - jnp.where(even, rows - NEAR_ROWS, 0)
    sent = (row_at >= 0) & (row_at < NEAR_ROWS) & (slot_ids < NEAR_SLOTS)
    sent_at = (slot_ids // share * NEAR_ROWS + row_at) * share + slot_ids % share
    far_live = jnp.where(even, live[0], live[2])
    code = jnp.where(sent & far_live, (2 << 10) + 1 + sent_at, code)
    ids = ids.reshape(rows, slots)
    own = jnp.where(live[1], (1 << 10) + 1 + ids, 0)
    near = jnp.where(even, live[2], live[0])
    near = jnp.where(near, (1 << 10) + 1 + span + ids, 0)
    codes = jnp.concatenate(
        [jnp.where(even, code, near), own, jnp.where(even, near, code)], axis=0
    )
    off3 = off.reshape(3 * rows, slots)
    at = lax.broadcasted_iota(jnp.int32, (1, 1, STRIDE), 2)
    table = jnp.sum(
        jnp.where(off3[:, :, None] + BAND == at, codes[:, :, None], 0), axis=1
    ).reshape(-1)
    table = jnp.concatenate([table, jnp.zeros((STRIDE,), jnp.int32)])
    place = jnp.where(
        live[1], jnp.arange(rows, dtype=jnp.int32)[:, None] + off[1], 3 * rows
    ).reshape(-1)
    start = jnp.full((8,), start_slot, jnp.int32)

    more = most_needed(columns, counts, layers) > FIRST
    acc, entries, size = local_products(
        start, table, place, blocks, inner, rows, slots, quarter
    )

    def second():
        late = pack(send_idx, blocks, FIRST, BOUND - FIRST)
        return lax.ppermute(late, ("row", "col"), outer_pairs)

    late = lax.cond(
        more, second, lambda: blank((BOUND - FIRST, edge, edge), values.dtype)
    )
    flags = jnp.stack([more.astype(jnp.int32), layer])
    square = far_products(
        flags, size, entries, acc, blocks, nears, outer, late, rows, quarter
    )
    return square.reshape(rows, quarter, edge, edge)


def solution(mesh):
    return jax.shard_map(
        per_device,
        mesh=mesh,
        in_specs=(P(("row", "col"), None, None, None), P(), P()),
        out_specs=P(("row", "col"), "layer", None, None),
        check_vma=False,
    )
```

```python
import functools

import jax
import jax.numpy as jnp
from jax import lax
from jax.experimental import pallas as pl
from jax.experimental.pallas import tpu as pltpu
from jax.sharding import PartitionSpec as P

BAND = 12
STRIDE = 64
WIDE = 16
UNROLL = 4
NEAR_ROWS = 6
NEAR_SLOTS = 12
FIRST = 60
BOUND = 132
ANY = pl.BlockSpec(memory_space=pl.ANY)
SMEM = pl.BlockSpec(memory_space=pltpu.SMEM)
VMEM = pl.BlockSpec(memory_space=pltpu.VMEM)


def pack_kernel(start, size, idx_ref, blocks_ref, out_ref, sem):
    def read(p, carry):
        pltpu.make_async_copy(
            blocks_ref.at[idx_ref[start + p]], out_ref.at[p], sem
        ).start()
        return carry

    lax.fori_loop(0, size, read, 0, unroll=4)
    pltpu.make_async_copy(blocks_ref.at[pl.ds(0, size)], out_ref, sem).wait()


def pack(idx, blocks, start, size):
    shape = (size,) + blocks.shape[1:]
    return pl.pallas_call(
        functools.partial(pack_kernel, start, size),
        out_shape=jax.ShapeDtypeStruct(shape, blocks.dtype),
        in_specs=[SMEM, ANY],
        out_specs=VMEM,
        scratch_shapes=[pltpu.SemaphoreType.DMA],
        compiler_params=pltpu.CompilerParams(vmem_limit_bytes=8 << 20),
        name="pack",
    )(idx, blocks)


def run_list(entries, length, a_ref, v_ref, acc_ref):
    def steps(begin, count, carry):
        parts = []
        for u in range(count):
            e0 = entries[(begin + u) * 2]
            e1 = entries[(begin + u) * 2 + 1]
            lhs = jnp.concatenate(
                [a_ref[(e0 >> 10) & 255], a_ref[(e1 >> 10) & 255]], axis=1
            )
            rhs = jnp.concatenate([v_ref[e0 & 1023], v_ref[e1 & 1023]], axis=0)
            parts.append(
                (e0 >> 18, jnp.dot(lhs, rhs, preferred_element_type=jnp.float32))
            )
        for out, part in parts:
            acc_ref[out] += part
        return carry

    pairs = length // 2
    wide = pairs // WIDE
    lax.fori_loop(0, wide, lambda t, c: steps(t * WIDE, WIDE, c), 0)
    rest = (pairs - wide * WIDE) // UNROLL
    lax.fori_loop(0, rest, lambda t, c: steps(wide * WIDE + t * UNROLL, UNROLL, c), 0)


def local_kernel(
    rows,
    slots,
    quarter,
    start_ref,
    table_ref,
    place_ref,
    blocks_ref,
    inner_ref,
    acc_ref,
    a_ref,
    near_ref,
    far_ref,
    size_ref,
    own_ref,
    inner_v,
    sem,
):
    count = rows * slots
    outs = rows * quarter
    size = 2 * UNROLL
    load = pltpu.make_async_copy(inner_ref, inner_v.at[pl.ds(1 + count, count)], sem.at[0])
    load.start()
    load_own = pltpu.make_async_copy(blocks_ref, inner_v.at[pl.ds(1, count)], sem.at[1])
    load_own.start()
    load_a = pltpu.make_async_copy(blocks_ref, a_ref, sem.at[2])
    load_a.start()
    inner_v[0] = jnp.zeros(inner_v.shape[1:], inner_v.dtype)

    def clear(o, carry):
        acc_ref[o] = jnp.zeros(acc_ref.shape[1:], acc_ref.dtype)
        return carry

    lax.fori_loop(0, outs + 1, clear, 0)
    start_slot = start_ref[0]

    def one_row(i, ends):
        base = i * slots
        row_tag = base << 10
        terms_at = [place_ref[base + m] * (STRIDE - 1) for m in range(slots)]

        def one_output(p, ends):
            j_at = place_ref[base + start_slot + p]
            tag = row_tag + ((i * quarter + p) << 18)

            def terms(ends):
                e_own, e_near, e_far = ends
                for m in range(slots):
                    code = table_ref[terms_at[m] + (j_at + 2 * BAND)]
                    entry = (code & 1023) + (tag + (m << 10))
                    own_ref[e_own] = entry
                    near_ref[e_near] = entry
                    far_ref[e_far] = entry
                    e_own += (code >> 10) & 1
                    e_near += (code >> 11) & 1
                    e_far += code >> 12
                own_ref[e_own] = tag
                near_ref[e_near] = tag
                far_ref[e_far] = tag
                return e_own + (e_own & 1), e_near + (e_near & 1), e_far + (e_far & 1)

            return lax.cond(j_at < 3 * rows, terms, lambda ends: ends, ends)

        return lax.fori_loop(0, quarter, one_output, ends)

    zero = jnp.int32(0)
    e_own, e_near, e_far = lax.fori_loop(0, rows, one_row, (zero, zero, zero))
    for u in range(size):
        own_ref[e_own + u] = outs << 18
        near_ref[e_near + u] = outs << 18
        far_ref[e_far + u] = outs << 18
    size_ref[0] = (e_near + size - 1) // size * size
    size_ref[1] = (e_far + size - 1) // size * size
    load_own.wait()
    load_a.wait()
    load.wait()
    run_list(own_ref, (e_own + size - 1) // size * size, a_ref, inner_v, acc_ref)


def local_products(start, table, place, blocks, inner, rows, slots, quarter):
    edge = blocks.shape[-1]
    outs = rows * quarter
    length = outs * slots + 4 * UNROLL
    return pl.pallas_call(
        functools.partial(local_kernel, rows, slots, quarter),
        out_shape=(
            jax.ShapeDtypeStruct((outs + 1, edge, edge), jnp.float32),
            jax.ShapeDtypeStruct(blocks.shape, blocks.dtype),
            jax.ShapeDtypeStruct((length,), jnp.int32),
            jax.ShapeDtypeStruct((length,), jnp.int32),
            jax.ShapeDtypeStruct((8,), jnp.int32),
        ),
        in_specs=[SMEM, SMEM, SMEM, ANY, ANY],
        out_specs=(VMEM, VMEM, SMEM, SMEM, SMEM),
        scratch_shapes=[
            pltpu.SMEM((length,), jnp.int32),
            pltpu.VMEM((2 * rows * slots + 1, edge, edge), blocks.dtype),
            pltpu.SemaphoreType.DMA((3,)),
        ],
        compiler_params=pltpu.CompilerParams(vmem_limit_bytes=32 << 20),
        cost_estimate=pl.CostEstimate(
            flops=10 * 10**9, bytes_accessed=24 * 10**6, transcendentals=0
        ),
        name="local_products",
    )(start, table, place, blocks, inner)


def near_kernel(
    layer_ref,
    size_ref,
    list_ref,
    acc_in,
    a_ref,
    near0_ref,
    near1_ref,
    near2_ref,
    near3_ref,
    acc_ref,
    v_ref,
    sem,
):
    nears = (near0_ref, near1_ref, near2_ref, near3_ref)
    near = near0_ref.shape[0]
    copies = []
    for away, ref in enumerate(nears):
        source = lax.rem(layer_ref[0] + len(nears) - away, len(nears))
        copies.append(
            pltpu.make_async_copy(
                ref, v_ref.at[pl.ds(1 + source * near, near)], sem.at[away]
            )
        )
    for copy in copies:
        copy.start()
    v_ref[0] = jnp.zeros(v_ref.shape[1:], v_ref.dtype)
    for copy in copies:
        copy.wait()
    run_list(list_ref, size_ref[0], a_ref, v_ref, acc_ref)


def near_products(layer, size, entries, acc, blocks, nears):
    edge = blocks.shape[-1]
    held = 1 + len(nears) * nears[0].shape[0]
    return pl.pallas_call(
        near_kernel,
        out_shape=jax.ShapeDtypeStruct(acc.shape, acc.dtype),
        in_specs=[SMEM] * 3 + [VMEM, VMEM] + [ANY] * len(nears),
        out_specs=VMEM,
        scratch_shapes=[
            pltpu.VMEM((held, edge, edge), blocks.dtype),
            pltpu.SemaphoreType.DMA((len(nears),)),
        ],
        input_output_aliases={3: 0},
        compiler_params=pltpu.CompilerParams(vmem_limit_bytes=24 << 20),
        name="near_products",
    )(layer, size, entries, acc, blocks, *nears)


def far_kernel(
    rows,
    quarter,
    more_ref,
    size_ref,
    list_ref,
    acc_in,
    a_ref,
    first_ref,
    late_ref,
    out_ref,
    acc_ref,
    v_ref,
    held,
    sem,
):
    first, late = first_ref.shape[0], late_ref.shape[0]
    load = pltpu.make_async_copy(first_ref, v_ref.at[pl.ds(1, first)], sem.at[0])
    load.start()
    v_ref[0] = jnp.zeros(v_ref.shape[1:], v_ref.dtype)

    @pl.when(more_ref[0] > 0)
    def _():
        late_copy = pltpu.make_async_copy(
            late_ref, v_ref.at[pl.ds(1 + first, late)], sem.at[1]
        )
        late_copy.start()
        late_copy.wait()

    load.wait()
    run_list(list_ref, size_ref[1], a_ref, v_ref, acc_ref)

    def finish(i, carry):
        part = pl.ds(i * quarter, quarter)
        held[part] = acc_ref[part].astype(held.dtype)
        pltpu.make_async_copy(held.at[part], out_ref.at[part], sem.at[2]).start()
        return carry

    lax.fori_loop(0, rows, finish, 0)
    pltpu.make_async_copy(held, out_ref, sem.at[2]).wait()


def far_products(more, size, entries, acc, blocks, first, late, rows, quarter):
    edge = blocks.shape[-1]
    outs = rows * quarter
    held = 1 + first.shape[0] + late.shape[0]
    square, _ = pl.pallas_call(
        functools.partial(far_kernel, rows, quarter),
        out_shape=(
            jax.ShapeDtypeStruct((outs, edge, edge), blocks.dtype),
            jax.ShapeDtypeStruct(acc.shape, acc.dtype),
        ),
        in_specs=[SMEM] * 3 + [VMEM, VMEM, ANY, ANY],
        out_specs=(ANY, VMEM),
        scratch_shapes=[
            pltpu.VMEM((held, edge, edge), blocks.dtype),
            pltpu.VMEM((outs, edge, edge), blocks.dtype),
            pltpu.SemaphoreType.DMA((3,)),
        ],
        input_output_aliases={3: 1},
        compiler_params=pltpu.CompilerParams(vmem_limit_bytes=24 << 20),
        name="far_products",
    )(more, size, entries, acc, blocks, first, late)
    return square


def blank(shape, dtype):
    return pl.pallas_call(
        lambda out_ref: None,
        out_shape=jax.ShapeDtypeStruct(shape, dtype),
        out_specs=ANY,
        name="blank",
    )()


def or_reduce(x, axis):
    return lax.reduce(x, jnp.uint32(0), lax.bitwise_or, (axis,))


def bit_masks(off, live):
    bits = jnp.where(live, jnp.uint32(1) << off.astype(jnp.uint32), jnp.uint32(0))
    return or_reduce(bits, 1), bits


def needed(k_mask, i_mask, i_part, later):
    rows = k_mask.shape[-1]
    kk = lax.broadcasted_iota(jnp.int32, (rows, rows), 0)
    ii = lax.broadcasted_iota(jnp.int32, (rows, rows), 1)
    ahead = ii - kk if later else kk - ii
    valid = ahead <= 0
    shift = jnp.where(valid, rows + ahead, 0).astype(jnp.uint32)
    at = BAND - shift if later else BAND + shift
    has = valid & (((i_mask[..., None, :] >> at) & 1) == 1)
    moved = i_part[..., None, :] << shift if later else i_part[..., None, :] >> shift
    return k_mask & or_reduce(jnp.where(has, moved, jnp.uint32(0)), moved.ndim - 1)


def most_needed(columns, counts, layers):
    total_rows, slots = columns.shape
    quarter = slots // layers
    rows_id = jnp.arange(total_rows, dtype=jnp.int32)
    off = (columns - rows_id[:, None] + BAND) % total_rows
    slot_ids = jnp.arange(slots, dtype=jnp.int32)
    live = slot_ids[None, :] < counts[:, None]
    mask, bits = bit_masks(off, live)
    part = jnp.stack(
        [or_reduce(bits[:, q * quarter : (q + 1) * quarter], 1) for q in range(layers)]
    )
    mask_wrap = jnp.concatenate([mask[-BAND:], mask, mask[:BAND]])
    part_wrap = jnp.concatenate([part[:, -BAND:], part, part[:, :BAND]], axis=1)
    kk = rows_id % BAND
    up = jnp.zeros_like(part)
    down = jnp.zeros_like(part)
    for s in range(1, BAND + 1):
        i_mask = mask_wrap[BAND + s : BAND + s + total_rows]
        i_part = part_wrap[:, BAND + s : BAND + s + total_rows]
        has = (((i_mask >> (BAND - s)) & 1) == 1) & (kk + s >= BAND)
        up = up | jnp.where(has, i_part << s, jnp.uint32(0))
        i_mask = mask_wrap[BAND - s : BAND - s + total_rows]
        i_part = part_wrap[:, BAND - s : BAND - s + total_rows]
        has = (((i_mask >> (BAND + s)) & 1) == 1) & (kk - s < 0)
        down = down | jnp.where(has, i_part >> s, jnp.uint32(0))
    odd = (rows_id // BAND) % 2 == 1
    fixed = or_reduce(bits[:, :NEAR_SLOTS], 1)
    close = jnp.where(odd, kk >= BAND - NEAR_ROWS, kk < NEAR_ROWS)
    asked = jnp.where(odd, up, down) & mask & jnp.where(close, ~fixed, ~jnp.uint32(0))
    per_row = lax.population_count(asked).astype(jnp.bfloat16)
    member = rows_id[:, None] // BAND == jnp.arange(total_rows // BAND)[None, :]
    per_group = jnp.dot(
        per_row, member.astype(jnp.bfloat16), preferred_element_type=jnp.float32
    )
    return jnp.max(per_group)


def per_device(values, columns, counts):
    rows, slots, edge, _ = values.shape
    layers = lax.axis_size("layer")
    quarter = slots // layers
    start_slot = lax.axis_index("layer") * quarter
    total_rows = columns.shape[0]
    group = lax.axis_index(("row", "col"))
    groups = lax.axis_size(("row", "col"))
    even = group % 2 == 0
    first_row = group * rows
    blocks = values.reshape((-1, edge, edge))
    span = rows * slots

    inner = lax.ppermute(blocks, ("row", "col"), [(g, g ^ 1) for g in range(groups)])

    share = NEAR_SLOTS // layers
    layer = lax.axis_index("layer")
    outer_pairs = [
        (g, (g - 1) % groups if g % 2 == 0 else (g + 1) % groups) for g in range(groups)
    ]
    near_rows = lax.dynamic_slice(
        values,
        (jnp.where(even, 0, rows - NEAR_ROWS), layer * share, 0, 0),
        (NEAR_ROWS, share, edge, edge),
    ).reshape(-1, edge, edge)
    near_mine = lax.ppermute(near_rows, ("row", "col"), outer_pairs)
    both = jnp.concatenate([columns.T, counts[None, :]], axis=0)
    both = lax.optimization_barrier(both)
    both = jnp.concatenate([both[:, -rows:], both, both[:, :rows]], axis=1)
    both = lax.dynamic_slice_in_dim(both, first_row, 3 * rows, 1)
    cols, cnts = both[:slots].T, both[slots]
    row_ids = first_row - rows + jnp.arange(3 * rows, dtype=jnp.int32)
    off = (cols - row_ids[:, None] + BAND) % total_rows
    slot_ids = jnp.arange(slots, dtype=jnp.int32)[None, :]
    live = slot_ids < cnts[:, None]
    mask, bits = bit_masks(off, live)
    mine = (slot_ids >= start_slot) & (slot_ids < start_slot + quarter)
    part = or_reduce(jnp.where(mine, bits, jnp.uint32(0)), 1)
    mask = mask.reshape(3, rows)
    part = part.reshape(3, rows)
    off = off.reshape(3, rows, slots)
    live = live.reshape(3, rows, slots)

    def pair(x):
        return jnp.where(even, x[:2], x[1:])

    mask2, part2, off2, live2 = pair(mask), pair(part), pair(off), pair(live)
    ask = jnp.stack(
        [
            needed(mask2[0], mask2[1], part2[1], True),
            needed(mask2[1], mask2[0], part2[0], False),
        ]
    )
    need = (((ask[:, :, None] >> off2.astype(jnp.uint32)) & 1) == 1) & live2
    fixed = (jnp.arange(rows)[:, None] < NEAR_ROWS) & (slot_ids < NEAR_SLOTS)
    need = jnp.stack([need[0, ::-1], need[1]]) & ~fixed
    need = need.reshape(2, span)
    before = (
        lax.broadcasted_iota(jnp.int32, (span, span), 0)
        < lax.broadcasted_iota(jnp.int32, (span, span), 1)
    ).astype(jnp.bfloat16)
    pos = jnp.dot(
        need.astype(jnp.bfloat16), before, preferred_element_type=jnp.float32
    ).astype(jnp.int32)
    ids = jnp.arange(span, dtype=jnp.int32)
    ids_up = (rows - 1 - ids // slots) * slots + ids % slots
    give, give_pos = jnp.where(even, need[1], need[0]), jnp.where(even, pos[1], pos[0])
    give_ids = jnp.where(even, ids, ids_up)
    get, get_pos = jnp.where(even, need[0], need[1]), jnp.where(even, pos[0], pos[1])
    hit = give[:, None] & (
        give_pos[:, None] == jnp.arange(BOUND, dtype=jnp.int32)[None, :]
    )
    send_idx = jnp.sum(jnp.where(hit, give_ids[:, None], 0), axis=0)

    send_idx, near_mine = lax.optimization_barrier((send_idx, near_mine))
    nears = [near_mine] + [
        lax.ppermute(near_mine, "layer", [(x, (x + d) % layers) for x in range(layers)])
        for d in range(1, layers)
    ]
    packed = pack(send_idx, blocks, 0, FIRST)
    outer = lax.ppermute(packed, ("row", "col"), outer_pairs)

    code = jnp.where(get, (4 << 10) + 1 + get_pos, 0)
    code = jnp.where(even, code.reshape(rows, slots)[::-1], code.reshape(rows, slots))
    row_at = jnp.arange(rows, dtype=jnp.int32)[:, None] - jnp.where(even, rows - NEAR_ROWS, 0)
    sent = (row_at >= 0) & (row_at < NEAR_ROWS) & (slot_ids < NEAR_SLOTS)
    sent_at = (slot_ids // share * NEAR_ROWS + row_at) * share + slot_ids % share
    far_live = jnp.where(even, live[0], live[2])
    code = jnp.where(sent & far_live, (2 << 10) + 1 + sent_at, code)
    ids = ids.reshape(rows, slots)
    own = jnp.where(live[1], (1 << 10) + 1 + ids, 0)
    near = jnp.where(even, live[2], live[0])
    near = jnp.where(near, (1 << 10) + 1 + span + ids, 0)
    codes = jnp.concatenate(
        [jnp.where(even, code, near), own, jnp.where(even, near, code)], axis=0
    )
    off3 = off.reshape(3 * rows, slots)
    at = lax.broadcasted_iota(jnp.int32, (1, 1, STRIDE), 2)
    table = jnp.sum(
        jnp.where(off3[:, :, None] + BAND == at, codes[:, :, None], 0), axis=1
    ).reshape(-1)
    table = jnp.concatenate([table, jnp.zeros((STRIDE,), jnp.int32)])
    place = jnp.where(
        live[1], jnp.arange(rows, dtype=jnp.int32)[:, None] + off[1], 3 * rows
    ).reshape(-1)
    start = jnp.full((8,), start_slot, jnp.int32)

    acc, held, near_list, far_list, size = local_products(
        start, table, place, blocks, inner, rows, slots, quarter
    )
    columns, counts, size = lax.optimization_barrier((columns, counts, size))
    more = most_needed(columns, counts, layers) > FIRST

    def second():
        late = pack(send_idx, blocks, FIRST, BOUND - FIRST)
        return lax.ppermute(late, ("row", "col"), outer_pairs)

    late = lax.cond(
        more, second, lambda: blank((BOUND - FIRST, edge, edge), values.dtype)
    )
    acc = near_products(jnp.full((8,), layer, jnp.int32), size, near_list, acc, held, nears)
    more = jnp.full((8,), more, jnp.int32)
    square = far_products(more, size, far_list, acc, held, outer, late, rows, quarter)
    return square.reshape(rows, quarter, edge, edge)


def solution(mesh):
    return jax.shard_map(
        per_device,
        mesh=mesh,
        in_specs=(P(("row", "col"), None, None, None), P(), P()),
        out_specs=P(("row", "col"), "layer", None, None),
        check_vma=False,
    )
```

```python
import functools

import jax
import jax.numpy as jnp
from jax import lax
from jax.experimental import pallas as pl
from jax.experimental.pallas import tpu as pltpu
from jax.sharding import PartitionSpec as P

BAND = 12
STRIDE = 64
WIDE = 16
UNROLL = 4
NEAR_ROWS = 6
NEAR_SLOTS = 12
FIRST = 60
BOUND = 132
ANY = pl.BlockSpec(memory_space=pl.ANY)
SMEM = pl.BlockSpec(memory_space=pltpu.SMEM)
VMEM = pl.BlockSpec(memory_space=pltpu.VMEM)


def pack_kernel(start, size, idx_ref, blocks_ref, out_ref, sem):
    def read(p, carry):
        pltpu.make_async_copy(
            blocks_ref.at[idx_ref[start + p]], out_ref.at[p], sem
        ).start()
        return carry

    lax.fori_loop(0, size, read, 0, unroll=4)
    pltpu.make_async_copy(blocks_ref.at[pl.ds(0, size)], out_ref, sem).wait()


def pack(idx, blocks, start, size):
    shape = (size,) + blocks.shape[1:]
    return pl.pallas_call(
        functools.partial(pack_kernel, start, size),
        out_shape=jax.ShapeDtypeStruct(shape, blocks.dtype),
        in_specs=[SMEM, ANY],
        out_specs=VMEM,
        scratch_shapes=[pltpu.SemaphoreType.DMA],
        compiler_params=pltpu.CompilerParams(vmem_limit_bytes=8 << 20),
        name="pack",
    )(idx, blocks)


def run_list(entries, length, a_ref, v_ref, acc_ref):
    def steps(begin, count, carry):
        parts = []
        for u in range(count):
            e0 = entries[(begin + u) * 2]
            e1 = entries[(begin + u) * 2 + 1]
            lhs = jnp.concatenate(
                [a_ref[(e0 >> 10) & 255], a_ref[(e1 >> 10) & 255]], axis=1
            )
            rhs = jnp.concatenate([v_ref[e0 & 1023], v_ref[e1 & 1023]], axis=0)
            parts.append(
                (e0 >> 18, jnp.dot(lhs, rhs, preferred_element_type=jnp.float32))
            )
        for out, part in parts:
            acc_ref[out] += part
        return carry

    pairs = length // 2
    wide = pairs // WIDE
    lax.fori_loop(0, wide, lambda t, c: steps(t * WIDE, WIDE, c), 0)
    rest = (pairs - wide * WIDE) // UNROLL
    lax.fori_loop(0, rest, lambda t, c: steps(wide * WIDE + t * UNROLL, UNROLL, c), 0)


def local_kernel(
    rows,
    slots,
    quarter,
    start_ref,
    table_ref,
    place_ref,
    blocks_ref,
    inner_ref,
    acc_ref,
    a_ref,
    near_ref,
    far_ref,
    size_ref,
    own_ref,
    inner_v,
    sem,
):
    count = rows * slots
    outs = rows * quarter
    size = 2 * UNROLL
    load = pltpu.make_async_copy(inner_ref, inner_v.at[pl.ds(1 + count, count)], sem.at[0])
    load.start()
    load_own = pltpu.make_async_copy(blocks_ref, inner_v.at[pl.ds(1, count)], sem.at[1])
    load_own.start()
    load_a = pltpu.make_async_copy(blocks_ref, a_ref, sem.at[2])
    load_a.start()
    inner_v[0] = jnp.zeros(inner_v.shape[1:], inner_v.dtype)

    def clear(o, carry):
        acc_ref[o] = jnp.zeros(acc_ref.shape[1:], acc_ref.dtype)
        return carry

    lax.fori_loop(0, outs + 1, clear, 0)
    start_slot = start_ref[0]

    def one_row(i, ends):
        base = i * slots
        row_tag = base << 10
        terms_at = [place_ref[base + m] * (STRIDE - 1) for m in range(slots)]

        def one_output(p, ends):
            j_at = place_ref[base + start_slot + p]
            tag = row_tag + ((i * quarter + p) << 18)

            def terms(ends):
                e_own, e_near, e_far = ends
                for m in range(slots):
                    code = table_ref[terms_at[m] + (j_at + 2 * BAND)]
                    entry = (code & 1023) + (tag + (m << 10))
                    own_ref[e_own] = entry
                    near_ref[e_near] = entry
                    far_ref[e_far] = entry
                    e_own += (code >> 10) & 1
                    e_near += (code >> 11) & 1
                    e_far += code >> 12
                own_ref[e_own] = tag
                near_ref[e_near] = tag
                far_ref[e_far] = tag
                return e_own + (e_own & 1), e_near + (e_near & 1), e_far + (e_far & 1)

            return lax.cond(j_at < 3 * rows, terms, lambda ends: ends, ends)

        return lax.fori_loop(0, quarter, one_output, ends)

    zero = jnp.int32(0)
    e_own, e_near, e_far = lax.fori_loop(0, rows, one_row, (zero, zero, zero))
    for u in range(size):
        own_ref[e_own + u] = outs << 18
        near_ref[e_near + u] = outs << 18
        far_ref[e_far + u] = outs << 18
    size_ref[0] = (e_near + size - 1) // size * size
    size_ref[1] = (e_far + size - 1) // size * size
    load_own.wait()
    load_a.wait()
    load.wait()
    run_list(own_ref, (e_own + size - 1) // size * size, a_ref, inner_v, acc_ref)


def local_products(start, table, place, blocks, inner, rows, slots, quarter):
    edge = blocks.shape[-1]
    outs = rows * quarter
    length = outs * slots + 4 * UNROLL
    return pl.pallas_call(
        functools.partial(local_kernel, rows, slots, quarter),
        out_shape=(
            jax.ShapeDtypeStruct((outs + 1, edge, edge), jnp.float32),
            jax.ShapeDtypeStruct(blocks.shape, blocks.dtype),
            jax.ShapeDtypeStruct((length,), jnp.int32),
            jax.ShapeDtypeStruct((length,), jnp.int32),
            jax.ShapeDtypeStruct((8,), jnp.int32),
        ),
        in_specs=[SMEM, SMEM, SMEM, ANY, ANY],
        out_specs=(VMEM, VMEM, SMEM, SMEM, SMEM),
        scratch_shapes=[
            pltpu.SMEM((length,), jnp.int32),
            pltpu.VMEM((2 * rows * slots + 1, edge, edge), blocks.dtype),
            pltpu.SemaphoreType.DMA((3,)),
        ],
        compiler_params=pltpu.CompilerParams(vmem_limit_bytes=32 << 20),
        cost_estimate=pl.CostEstimate(
            flops=10 * 10**9, bytes_accessed=24 * 10**6, transcendentals=0
        ),
        name="local_products",
    )(start, table, place, blocks, inner)


def near_kernel(
    layer_ref,
    size_ref,
    list_ref,
    acc_in,
    a_ref,
    near0_ref,
    near1_ref,
    near2_ref,
    near3_ref,
    acc_ref,
    v_ref,
    sem,
):
    nears = (near0_ref, near1_ref, near2_ref, near3_ref)
    near = near0_ref.shape[0]
    copies = []
    for away, ref in enumerate(nears):
        source = lax.rem(layer_ref[0] + len(nears) - away, len(nears))
        copies.append(
            pltpu.make_async_copy(
                ref, v_ref.at[pl.ds(1 + source * near, near)], sem.at[away]
            )
        )
    for copy in copies:
        copy.start()
    v_ref[0] = jnp.zeros(v_ref.shape[1:], v_ref.dtype)
    for copy in copies:
        copy.wait()
    run_list(list_ref, size_ref[0], a_ref, v_ref, acc_ref)


def near_products(layer, size, entries, acc, blocks, nears):
    edge = blocks.shape[-1]
    held = 1 + len(nears) * nears[0].shape[0]
    return pl.pallas_call(
        near_kernel,
        out_shape=jax.ShapeDtypeStruct(acc.shape, acc.dtype),
        in_specs=[SMEM] * 3 + [VMEM, VMEM] + [ANY] * len(nears),
        out_specs=VMEM,
        scratch_shapes=[
            pltpu.VMEM((held, edge, edge), blocks.dtype),
            pltpu.SemaphoreType.DMA((len(nears),)),
        ],
        input_output_aliases={3: 0},
        compiler_params=pltpu.CompilerParams(vmem_limit_bytes=24 << 20),
        name="near_products",
    )(layer, size, entries, acc, blocks, *nears)


def far_kernel(
    rows,
    quarter,
    more_ref,
    size_ref,
    list_ref,
    acc_in,
    a_ref,
    first_ref,
    late_ref,
    out_ref,
    acc_ref,
    v_ref,
    held,
    sem,
):
    first, late = first_ref.shape[0], late_ref.shape[0]
    load = pltpu.make_async_copy(first_ref, v_ref.at[pl.ds(1, first)], sem.at[0])
    load.start()
    v_ref[0] = jnp.zeros(v_ref.shape[1:], v_ref.dtype)

    @pl.when(more_ref[0] > 0)
    def _():
        late_copy = pltpu.make_async_copy(
            late_ref, v_ref.at[pl.ds(1 + first, late)], sem.at[1]
        )
        late_copy.start()
        late_copy.wait()

    load.wait()
    run_list(list_ref, size_ref[1], a_ref, v_ref, acc_ref)

    def finish(i, carry):
        part = pl.ds(i * quarter, quarter)
        held[part] = acc_ref[part].astype(held.dtype)
        pltpu.make_async_copy(held.at[part], out_ref.at[part], sem.at[2]).start()
        return carry

    lax.fori_loop(0, rows, finish, 0)
    pltpu.make_async_copy(held, out_ref, sem.at[2]).wait()


def far_products(more, size, entries, acc, blocks, first, late, rows, quarter):
    edge = blocks.shape[-1]
    outs = rows * quarter
    held = 1 + first.shape[0] + late.shape[0]
    square, _ = pl.pallas_call(
        functools.partial(far_kernel, rows, quarter),
        out_shape=(
            jax.ShapeDtypeStruct((outs, edge, edge), blocks.dtype),
            jax.ShapeDtypeStruct(acc.shape, acc.dtype),
        ),
        in_specs=[SMEM] * 3 + [VMEM, VMEM, ANY, ANY],
        out_specs=(ANY, VMEM),
        scratch_shapes=[
            pltpu.VMEM((held, edge, edge), blocks.dtype),
            pltpu.VMEM((outs, edge, edge), blocks.dtype),
            pltpu.SemaphoreType.DMA((3,)),
        ],
        input_output_aliases={3: 1},
        compiler_params=pltpu.CompilerParams(vmem_limit_bytes=24 << 20),
        name="far_products",
    )(more, size, entries, acc, blocks, first, late)
    return square


def blank(shape, dtype):
    return pl.pallas_call(
        lambda out_ref: None,
        out_shape=jax.ShapeDtypeStruct(shape, dtype),
        out_specs=ANY,
        name="blank",
    )()


def or_reduce(x, axis):
    return lax.reduce(x, jnp.uint32(0), lax.bitwise_or, (axis,))


def bit_masks(off, live):
    bits = jnp.where(live, jnp.uint32(1) << off.astype(jnp.uint32), jnp.uint32(0))
    return or_reduce(bits, 1), bits


def needed(k_mask, i_mask, i_part, later):
    rows = k_mask.shape[-1]
    kk = lax.broadcasted_iota(jnp.int32, (rows, rows), 0)
    ii = lax.broadcasted_iota(jnp.int32, (rows, rows), 1)
    ahead = ii - kk if later else kk - ii
    valid = ahead <= 0
    shift = jnp.where(valid, rows + ahead, 0).astype(jnp.uint32)
    at = BAND - shift if later else BAND + shift
    has = valid & (((i_mask[..., None, :] >> at) & 1) == 1)
    moved = i_part[..., None, :] << shift if later else i_part[..., None, :] >> shift
    return k_mask & or_reduce(jnp.where(has, moved, jnp.uint32(0)), moved.ndim - 1)


def most_needed(columns, counts, layers):
    total_rows, slots = columns.shape
    quarter = slots // layers
    rows_id = jnp.arange(total_rows, dtype=jnp.int32)
    off = (columns - rows_id[:, None] + BAND) % total_rows
    slot_ids = jnp.arange(slots, dtype=jnp.int32)
    live = slot_ids[None, :] < counts[:, None]
    mask, bits = bit_masks(off, live)
    part = jnp.stack(
        [or_reduce(bits[:, q * quarter : (q + 1) * quarter], 1) for q in range(layers)]
    )
    mask_wrap = jnp.concatenate([mask[-BAND:], mask, mask[:BAND]])
    part_wrap = jnp.concatenate([part[:, -BAND:], part, part[:, :BAND]], axis=1)
    kk = rows_id % BAND
    up = jnp.zeros_like(part)
    down = jnp.zeros_like(part)
    for s in range(1, BAND + 1):
        i_mask = mask_wrap[BAND + s : BAND + s + total_rows]
        i_part = part_wrap[:, BAND + s : BAND + s + total_rows]
        has = (((i_mask >> (BAND - s)) & 1) == 1) & (kk + s >= BAND)
        up = up | jnp.where(has, i_part << s, jnp.uint32(0))
        i_mask = mask_wrap[BAND - s : BAND - s + total_rows]
        i_part = part_wrap[:, BAND - s : BAND - s + total_rows]
        has = (((i_mask >> (BAND + s)) & 1) == 1) & (kk - s < 0)
        down = down | jnp.where(has, i_part >> s, jnp.uint32(0))
    odd = (rows_id // BAND) % 2 == 1
    fixed = or_reduce(bits[:, :NEAR_SLOTS], 1)
    close = jnp.where(odd, kk >= BAND - NEAR_ROWS, kk < NEAR_ROWS)
    asked = jnp.where(odd, up, down) & mask & jnp.where(close, ~fixed, ~jnp.uint32(0))
    per_row = lax.population_count(asked).astype(jnp.bfloat16)
    member = rows_id[:, None] // BAND == jnp.arange(total_rows // BAND)[None, :]
    per_group = jnp.dot(
        per_row, member.astype(jnp.bfloat16), preferred_element_type=jnp.float32
    )
    return jnp.max(per_group)


def per_device(values, columns, counts):
    rows, slots, edge, _ = values.shape
    layers = lax.axis_size("layer")
    quarter = slots // layers
    start_slot = lax.axis_index("layer") * quarter
    total_rows = columns.shape[0]
    group = lax.axis_index(("row", "col"))
    groups = lax.axis_size(("row", "col"))
    even = group % 2 == 0
    first_row = group * rows
    blocks = values.reshape((-1, edge, edge))
    span = rows * slots

    inner = lax.ppermute(blocks, ("row", "col"), [(g, g ^ 1) for g in range(groups)])

    share = NEAR_SLOTS // layers
    layer = lax.axis_index("layer")
    outer_pairs = [
        (g, (g - 1) % groups if g % 2 == 0 else (g + 1) % groups) for g in range(groups)
    ]
    near_rows = lax.dynamic_slice(
        values,
        (jnp.where(even, 0, rows - NEAR_ROWS), layer * share, 0, 0),
        (NEAR_ROWS, share, edge, edge),
    ).reshape(-1, edge, edge)
    near_mine = lax.ppermute(near_rows, ("row", "col"), outer_pairs)
    both = jnp.concatenate([columns.T, counts[None, :]], axis=0)
    both = lax.optimization_barrier(both)
    both = jnp.concatenate([both[:, -rows:], both, both[:, :rows]], axis=1)
    both = lax.dynamic_slice_in_dim(both, first_row, 3 * rows, 1)
    cols, cnts = both[:slots].T, both[slots]
    row_ids = first_row - rows + jnp.arange(3 * rows, dtype=jnp.int32)
    off = (cols - row_ids[:, None] + BAND) % total_rows
    slot_ids = jnp.arange(slots, dtype=jnp.int32)[None, :]
    live = slot_ids < cnts[:, None]
    mask, bits = bit_masks(off, live)
    mine = (slot_ids >= start_slot) & (slot_ids < start_slot + quarter)
    part = or_reduce(jnp.where(mine, bits, jnp.uint32(0)), 1)
    mask = mask.reshape(3, rows)
    part = part.reshape(3, rows)
    off = off.reshape(3, rows, slots)
    live = live.reshape(3, rows, slots)

    def pair(x):
        return jnp.where(even, x[:2], x[1:])

    mask2, part2, off2, live2 = pair(mask), pair(part), pair(off), pair(live)
    ask = jnp.stack(
        [
            needed(mask2[0], mask2[1], part2[1], True),
            needed(mask2[1], mask2[0], part2[0], False),
        ]
    )
    need = (((ask[:, :, None] >> off2.astype(jnp.uint32)) & 1) == 1) & live2
    fixed = (jnp.arange(rows)[:, None] < NEAR_ROWS) & (slot_ids < NEAR_SLOTS)
    need = jnp.stack([need[0, ::-1], need[1]]) & ~fixed
    need = need.reshape(2, span)
    before = (
        lax.broadcasted_iota(jnp.int32, (span, span), 0)
        < lax.broadcasted_iota(jnp.int32, (span, span), 1)
    ).astype(jnp.bfloat16)
    pos = jnp.dot(
        need.astype(jnp.bfloat16), before, preferred_element_type=jnp.float32
    ).astype(jnp.int32)
    ids = jnp.arange(span, dtype=jnp.int32)
    ids_up = (rows - 1 - ids // slots) * slots + ids % slots
    give, give_pos = jnp.where(even, need[1], need[0]), jnp.where(even, pos[1], pos[0])
    give_ids = jnp.where(even, ids, ids_up)
    get, get_pos = jnp.where(even, need[0], need[1]), jnp.where(even, pos[0], pos[1])
    hit = give[:, None] & (
        give_pos[:, None] == jnp.arange(BOUND, dtype=jnp.int32)[None, :]
    )
    send_idx = jnp.sum(jnp.where(hit, give_ids[:, None], 0), axis=0)

    send_idx, near_mine = lax.optimization_barrier((send_idx, near_mine))
    nears = [near_mine] + [
        lax.ppermute(near_mine, "layer", [(x, (x + d) % layers) for x in range(layers)])
        for d in range(1, layers)
    ]
    packed = pack(send_idx, blocks, 0, FIRST)
    outer = lax.ppermute(packed, ("row", "col"), outer_pairs)

    code = jnp.where(get, (4 << 10) + 1 + get_pos, 0)
    code = jnp.where(even, code.reshape(rows, slots)[::-1], code.reshape(rows, slots))
    row_at = jnp.arange(rows, dtype=jnp.int32)[:, None] - jnp.where(even, rows - NEAR_ROWS, 0)
    sent = (row_at >= 0) & (row_at < NEAR_ROWS) & (slot_ids < NEAR_SLOTS)
    sent_at = (slot_ids // share * NEAR_ROWS + row_at) * share + slot_ids % share
    far_live = jnp.where(even, live[0], live[2])
    code = jnp.where(sent & far_live, (2 << 10) + 1 + sent_at, code)
    ids = ids.reshape(rows, slots)
    own = jnp.where(live[1], (1 << 10) + 1 + ids, 0)
    near = jnp.where(even, live[2], live[0])
    near = jnp.where(near, (1 << 10) + 1 + span + ids, 0)
    codes = jnp.concatenate(
        [jnp.where(even, code, near), own, jnp.where(even, near, code)], axis=0
    )
    off3 = off.reshape(3 * rows, slots)
    at = lax.broadcasted_iota(jnp.int32, (1, 1, STRIDE), 2)
    table = jnp.sum(
        jnp.where(off3[:, :, None] + BAND == at, codes[:, :, None], 0), axis=1
    ).reshape(-1)
    table = jnp.concatenate([table, jnp.zeros((STRIDE,), jnp.int32)])
    place = jnp.where(
        live[1], jnp.arange(rows, dtype=jnp.int32)[:, None] + off[1], 3 * rows
    ).reshape(-1)
    columns, counts, packed = lax.optimization_barrier((columns, counts, packed))
    more = most_needed(columns, counts, layers) > FIRST

    def second():
        late = pack(send_idx, blocks, FIRST, BOUND - FIRST)
        return lax.ppermute(late, ("row", "col"), outer_pairs)

    late = lax.cond(
        more, second, lambda: blank((BOUND - FIRST, edge, edge), values.dtype)
    )
    start = jnp.full((8,), start_slot, jnp.int32)

    acc, held, near_list, far_list, size = local_products(
        start, table, place, blocks, inner, rows, slots, quarter
    )
    acc = near_products(jnp.full((8,), layer, jnp.int32), size, near_list, acc, held, nears)
    more = jnp.full((8,), more, jnp.int32)
    square = far_products(more, size, far_list, acc, held, outer, late, rows, quarter)
    return square.reshape(rows, quarter, edge, edge)


def solution(mesh):
    return jax.shard_map(
        per_device,
        mesh=mesh,
        in_specs=(P(("row", "col"), None, None, None), P(), P()),
        out_specs=P(("row", "col"), "layer", None, None),
        check_vma=False,
    )
```

```python
import functools

import jax
import jax.numpy as jnp
import numpy as np
from jax import lax
from jax.experimental import pallas as pl
from jax.experimental.pallas import tpu as pltpu
from jax.sharding import PartitionSpec as P

BAND = 12
STRIDE = 64
WIDE = 16
UNROLL = 4
NEAR_ROWS = 6
NEAR_SLOTS = 12
FIRST = 60
BOUND = 132
ANY = pl.BlockSpec(memory_space=pl.ANY)
SMEM = pl.BlockSpec(memory_space=pltpu.SMEM)
VMEM = pl.BlockSpec(memory_space=pltpu.VMEM)


def pack_kernel(start, size, idx_ref, blocks_ref, out_ref, sem):
    def read(p, carry):
        pltpu.make_async_copy(
            blocks_ref.at[idx_ref[start + p]], out_ref.at[p], sem
        ).start()
        return carry

    lax.fori_loop(0, size, read, 0, unroll=4)
    pltpu.make_async_copy(blocks_ref.at[pl.ds(0, size)], out_ref, sem).wait()


def pack(idx, blocks, start, size):
    shape = (size,) + blocks.shape[1:]
    return pl.pallas_call(
        functools.partial(pack_kernel, start, size),
        out_shape=jax.ShapeDtypeStruct(shape, blocks.dtype),
        in_specs=[SMEM, ANY],
        out_specs=VMEM,
        scratch_shapes=[pltpu.SemaphoreType.DMA],
        compiler_params=pltpu.CompilerParams(vmem_limit_bytes=8 << 20),
        name="pack",
    )(idx, blocks)


def run_list(entries, length, a_ref, v_ref, acc_ref):
    def steps(begin, count, carry):
        parts = []
        for u in range(count):
            e0 = entries[(begin + u) * 2]
            e1 = entries[(begin + u) * 2 + 1]
            lhs = jnp.concatenate(
                [a_ref[(e0 >> 10) & 255], a_ref[(e1 >> 10) & 255]], axis=1
            )
            rhs = jnp.concatenate([v_ref[e0 & 1023], v_ref[e1 & 1023]], axis=0)
            parts.append(
                (e0 >> 18, jnp.dot(lhs, rhs, preferred_element_type=jnp.float32))
            )
        for out, part in parts:
            acc_ref[out] += part
        return carry

    pairs = length // 2
    wide = pairs // WIDE
    lax.fori_loop(0, wide, lambda t, c: steps(t * WIDE, WIDE, c), 0)
    rest = (pairs - wide * WIDE) // UNROLL
    lax.fori_loop(0, rest, lambda t, c: steps(wide * WIDE + t * UNROLL, UNROLL, c), 0)


def local_kernel(
    rows,
    slots,
    quarter,
    start_ref,
    table_ref,
    place_ref,
    blocks_ref,
    inner_ref,
    acc_ref,
    a_ref,
    near_ref,
    far_ref,
    size_ref,
    own_ref,
    inner_v,
    sem,
):
    count = rows * slots
    outs = rows * quarter
    size = 2 * UNROLL
    load = pltpu.make_async_copy(inner_ref, inner_v.at[pl.ds(count, count)], sem.at[0])
    load.start()
    load_own = pltpu.make_async_copy(blocks_ref, inner_v.at[pl.ds(0, count)], sem.at[1])
    load_own.start()
    load_a = pltpu.make_async_copy(blocks_ref, a_ref.at[pl.ds(0, count)], sem.at[2])
    load_a.start()
    a_ref[count] = jnp.zeros(a_ref.shape[1:], a_ref.dtype)

    def clear(o, carry):
        acc_ref[o] = jnp.zeros(acc_ref.shape[1:], acc_ref.dtype)
        return carry

    lax.fori_loop(0, outs + 1, clear, 0)
    start_slot = start_ref[0]

    def one_row(i, ends):
        base = i * slots
        row_tag = base << 10
        terms_at = [place_ref[base + m] * (STRIDE - 1) for m in range(slots)]

        def one_output(p, ends):
            j_at = place_ref[base + start_slot + p]
            tag = row_tag + ((i * quarter + p) << 18)

            def terms(ends):
                e_own, e_near, e_far = ends
                for m in range(slots):
                    code = table_ref[terms_at[m] + (j_at + 2 * BAND)]
                    entry = (code & 1023) + (tag + (m << 10))
                    own_ref[e_own] = entry
                    near_ref[e_near] = entry
                    far_ref[e_far] = entry
                    e_own += (code >> 10) & 1
                    e_near += (code >> 11) & 1
                    e_far += code >> 12
                none = ((i * quarter + p) << 18) | (count << 10)
                own_ref[e_own] = none
                near_ref[e_near] = none
                far_ref[e_far] = none
                return e_own + (e_own & 1), e_near + (e_near & 1), e_far + (e_far & 1)

            return lax.cond(j_at < 3 * rows, terms, lambda ends: ends, ends)

        return lax.fori_loop(0, quarter, one_output, ends)

    zero = jnp.int32(0)
    e_own, e_near, e_far = lax.fori_loop(0, rows, one_row, (zero, zero, zero))
    for u in range(size):
        none = (outs << 18) | (count << 10)
        own_ref[e_own + u] = none
        near_ref[e_near + u] = none
        far_ref[e_far + u] = none
    size_ref[0] = (e_near + size - 1) // size * size
    size_ref[1] = (e_far + size - 1) // size * size
    load_own.wait()
    load_a.wait()
    load.wait()
    run_list(own_ref, (e_own + size - 1) // size * size, a_ref, inner_v, acc_ref)


def local_products(start, table, place, blocks, inner, rows, slots, quarter):
    edge = blocks.shape[-1]
    outs = rows * quarter
    length = outs * slots + 4 * UNROLL
    return pl.pallas_call(
        functools.partial(local_kernel, rows, slots, quarter),
        out_shape=(
            jax.ShapeDtypeStruct((outs + 1, edge, edge), jnp.float32),
            jax.ShapeDtypeStruct((rows * slots + 1, edge, edge), blocks.dtype),
            jax.ShapeDtypeStruct((length,), jnp.int32),
            jax.ShapeDtypeStruct((length,), jnp.int32),
            jax.ShapeDtypeStruct((8,), jnp.int32),
        ),
        in_specs=[SMEM, SMEM, SMEM, ANY, ANY],
        out_specs=(VMEM, VMEM, SMEM, SMEM, SMEM),
        scratch_shapes=[
            pltpu.SMEM((length,), jnp.int32),
            pltpu.VMEM((2 * rows * slots, edge, edge), blocks.dtype),
            pltpu.SemaphoreType.DMA((3,)),
        ],
        compiler_params=pltpu.CompilerParams(vmem_limit_bytes=32 << 20),
        cost_estimate=pl.CostEstimate(
            flops=10 * 10**9, bytes_accessed=24 * 10**6, transcendentals=0
        ),
        name="local_products",
    )(start, table, place, blocks, inner)


def near_kernel(
    layer_ref,
    size_ref,
    list_ref,
    acc_in,
    a_ref,
    near0_ref,
    near1_ref,
    near2_ref,
    near3_ref,
    acc_ref,
    v_ref,
    sem,
):
    nears = (near0_ref, near1_ref, near2_ref, near3_ref)
    near = near0_ref.shape[0]
    copies = []
    for away, ref in enumerate(nears):
        source = lax.rem(layer_ref[0] + len(nears) - away, len(nears))
        copies.append(
            pltpu.make_async_copy(
                ref, v_ref.at[pl.ds(source * near, near)], sem.at[away]
            )
        )
    for copy in copies:
        copy.start()
    for copy in copies:
        copy.wait()
    run_list(list_ref, size_ref[0], a_ref, v_ref, acc_ref)


def near_products(layer, size, entries, acc, blocks, nears):
    edge = blocks.shape[-1]
    held = len(nears) * nears[0].shape[0]
    return pl.pallas_call(
        near_kernel,
        out_shape=jax.ShapeDtypeStruct(acc.shape, acc.dtype),
        in_specs=[SMEM] * 3 + [VMEM, VMEM] + [ANY] * len(nears),
        out_specs=VMEM,
        scratch_shapes=[
            pltpu.VMEM((held, edge, edge), blocks.dtype),
            pltpu.SemaphoreType.DMA((len(nears),)),
        ],
        input_output_aliases={3: 0},
        compiler_params=pltpu.CompilerParams(vmem_limit_bytes=24 << 20),
        name="near_products",
    )(layer, size, entries, acc, blocks, *nears)


def far_kernel(
    rows,
    quarter,
    more_ref,
    size_ref,
    list_ref,
    acc_in,
    a_ref,
    first_ref,
    late_ref,
    out_ref,
    acc_ref,
    v_ref,
    held,
    sem,
):
    first, late = first_ref.shape[0], late_ref.shape[0]

    @pl.when(more_ref[0] == 0)
    def _():
        run_list(list_ref, size_ref[1], a_ref, first_ref, acc_ref)

    @pl.when(more_ref[0] != 0)
    def _():
        late_copy = pltpu.make_async_copy(
            late_ref, v_ref.at[pl.ds(first, late)], sem.at[0]
        )
        late_copy.start()

        def move(b, carry):
            v_ref[b] = first_ref[b]
            return carry

        lax.fori_loop(0, first, move, 0)
        late_copy.wait()
        run_list(list_ref, size_ref[1], a_ref, v_ref, acc_ref)

    def finish(i, carry):
        part = pl.ds(i * quarter, quarter)
        held[part] = acc_ref[part].astype(held.dtype)
        pltpu.make_async_copy(held.at[part], out_ref.at[part], sem.at[1]).start()
        return carry

    lax.fori_loop(0, rows, finish, 0)
    pltpu.make_async_copy(held, out_ref, sem.at[1]).wait()


def far_products(more, size, entries, acc, blocks, first, late, rows, quarter):
    edge = blocks.shape[-1]
    outs = rows * quarter
    held = first.shape[0] + late.shape[0]
    square, _ = pl.pallas_call(
        functools.partial(far_kernel, rows, quarter),
        out_shape=(
            jax.ShapeDtypeStruct((outs, edge, edge), blocks.dtype),
            jax.ShapeDtypeStruct(acc.shape, acc.dtype),
        ),
        in_specs=[SMEM] * 3 + [VMEM, VMEM, VMEM, ANY],
        out_specs=(ANY, VMEM),
        scratch_shapes=[
            pltpu.VMEM((held, edge, edge), blocks.dtype),
            pltpu.VMEM((outs, edge, edge), blocks.dtype),
            pltpu.SemaphoreType.DMA((2,)),
        ],
        input_output_aliases={3: 1},
        compiler_params=pltpu.CompilerParams(vmem_limit_bytes=24 << 20),
        name="far_products",
    )(more, size, entries, acc, blocks, first, late)
    return square


def blank(shape, dtype):
    return pl.pallas_call(
        lambda out_ref: None,
        out_shape=jax.ShapeDtypeStruct(shape, dtype),
        out_specs=ANY,
        name="blank",
    )()


def or_reduce(x, axis):
    return lax.reduce(x, jnp.uint32(0), lax.bitwise_or, (axis,))


def bit_masks(off, live):
    bits = jnp.where(live, jnp.uint32(1) << off.astype(jnp.uint32), jnp.uint32(0))
    return or_reduce(bits, 1), bits


def needed(k_mask, i_mask, i_part, later):
    rows = k_mask.shape[-1]
    kk = lax.broadcasted_iota(jnp.int32, (rows, rows), 0)
    ii = lax.broadcasted_iota(jnp.int32, (rows, rows), 1)
    ahead = ii - kk if later else kk - ii
    valid = ahead <= 0
    shift = jnp.where(valid, rows + ahead, 0).astype(jnp.uint32)
    at = BAND - shift if later else BAND + shift
    has = valid & (((i_mask[..., None, :] >> at) & 1) == 1)
    moved = i_part[..., None, :] << shift if later else i_part[..., None, :] >> shift
    return k_mask & or_reduce(jnp.where(has, moved, jnp.uint32(0)), moved.ndim - 1)


def most_needed(columns, counts, layers):
    total_rows, slots = columns.shape
    quarter = slots // layers
    rows_id = jnp.arange(total_rows, dtype=jnp.int32)
    off = (columns - rows_id[:, None] + BAND) % total_rows
    slot_ids = jnp.arange(slots, dtype=jnp.int32)
    live = slot_ids[None, :] < counts[:, None]
    mask, bits = bit_masks(off, live)
    part = jnp.stack(
        [or_reduce(bits[:, q * quarter : (q + 1) * quarter], 1) for q in range(layers)]
    )
    mask_wrap = jnp.concatenate([mask[-BAND:], mask, mask[:BAND]])
    part_wrap = jnp.concatenate([part[:, -BAND:], part, part[:, :BAND]], axis=1)
    kk = rows_id % BAND
    up = jnp.zeros_like(part)
    down = jnp.zeros_like(part)
    for s in range(1, BAND + 1):
        i_mask = mask_wrap[BAND + s : BAND + s + total_rows]
        i_part = part_wrap[:, BAND + s : BAND + s + total_rows]
        has = (((i_mask >> (BAND - s)) & 1) == 1) & (kk + s >= BAND)
        up = up | jnp.where(has, i_part << s, jnp.uint32(0))
        i_mask = mask_wrap[BAND - s : BAND - s + total_rows]
        i_part = part_wrap[:, BAND - s : BAND - s + total_rows]
        has = (((i_mask >> (BAND + s)) & 1) == 1) & (kk - s < 0)
        down = down | jnp.where(has, i_part >> s, jnp.uint32(0))
    odd = (rows_id // BAND) % 2 == 1
    fixed = or_reduce(bits[:, :NEAR_SLOTS], 1)
    close = jnp.where(odd, kk >= BAND - NEAR_ROWS, kk < NEAR_ROWS)
    asked = jnp.where(odd, up, down) & mask & jnp.where(close, ~fixed, ~jnp.uint32(0))
    per_row = lax.population_count(asked).astype(jnp.bfloat16)
    member = np.arange(total_rows)[:, None] // BAND == np.arange(total_rows // BAND)
    per_group = jnp.dot(
        per_row, jnp.asarray(member, jnp.bfloat16), preferred_element_type=jnp.float32
    )
    return jnp.max(per_group)


def per_device(values, columns, counts):
    rows, slots, edge, _ = values.shape
    layers = lax.axis_size("layer")
    quarter = slots // layers
    start_slot = lax.axis_index("layer") * quarter
    total_rows = columns.shape[0]
    group = lax.axis_index(("row", "col"))
    groups = lax.axis_size(("row", "col"))
    even = group % 2 == 0
    first_row = group * rows
    blocks = values.reshape((-1, edge, edge))
    span = rows * slots

    inner = lax.ppermute(blocks, ("row", "col"), [(g, g ^ 1) for g in range(groups)])

    share = NEAR_SLOTS // layers
    layer = lax.axis_index("layer")
    outer_pairs = [
        (g, (g - 1) % groups if g % 2 == 0 else (g + 1) % groups) for g in range(groups)
    ]
    near_rows = lax.dynamic_slice(
        values,
        (jnp.where(even, 0, rows - NEAR_ROWS), layer * share, 0, 0),
        (NEAR_ROWS, share, edge, edge),
    ).reshape(-1, edge, edge)
    near_mine = lax.ppermute(near_rows, ("row", "col"), outer_pairs)
    both = jnp.concatenate([columns.T, counts[None, :]], axis=0)
    both = lax.optimization_barrier(both)
    both = jnp.concatenate([both[:, -rows:], both, both[:, :rows]], axis=1)
    both = lax.dynamic_slice_in_dim(both, first_row, 3 * rows, 1)
    cols, cnts = both[:slots].T, both[slots]
    row_ids = first_row - rows + jnp.arange(3 * rows, dtype=jnp.int32)
    off = (cols - row_ids[:, None] + BAND) % total_rows
    slot_ids = jnp.arange(slots, dtype=jnp.int32)[None, :]
    live = slot_ids < cnts[:, None]
    mask, bits = bit_masks(off, live)
    mine = (slot_ids >= start_slot) & (slot_ids < start_slot + quarter)
    part = or_reduce(jnp.where(mine, bits, jnp.uint32(0)), 1)
    mask = mask.reshape(3, rows)
    part = part.reshape(3, rows)
    off = off.reshape(3, rows, slots)
    live = live.reshape(3, rows, slots)

    def pair(x):
        return jnp.where(even, x[:2], x[1:])

    mask2, part2, off2, live2 = pair(mask), pair(part), pair(off), pair(live)
    ask = jnp.stack(
        [
            needed(mask2[0], mask2[1], part2[1], True),
            needed(mask2[1], mask2[0], part2[0], False),
        ]
    )
    need = (((ask[:, :, None] >> off2.astype(jnp.uint32)) & 1) == 1) & live2
    fixed = (jnp.arange(rows)[:, None] < NEAR_ROWS) & (slot_ids < NEAR_SLOTS)
    need = jnp.stack([need[0, ::-1], need[1]]) & ~fixed
    need = need.reshape(2, span)
    before = (
        lax.broadcasted_iota(jnp.int32, (span, span), 0)
        < lax.broadcasted_iota(jnp.int32, (span, span), 1)
    ).astype(jnp.bfloat16)
    pos = jnp.dot(
        need.astype(jnp.bfloat16), before, preferred_element_type=jnp.float32
    ).astype(jnp.int32)
    ids = jnp.arange(span, dtype=jnp.int32)
    ids_up = (rows - 1 - ids // slots) * slots + ids % slots
    give, give_pos = jnp.where(even, need[1], need[0]), jnp.where(even, pos[1], pos[0])
    give_ids = jnp.where(even, ids, ids_up)
    get, get_pos = jnp.where(even, need[0], need[1]), jnp.where(even, pos[0], pos[1])
    hit = give[:, None] & (
        give_pos[:, None] == jnp.arange(BOUND, dtype=jnp.int32)[None, :]
    )
    send_idx = jnp.sum(jnp.where(hit, give_ids[:, None], 0), axis=0)

    packed = pack(send_idx, blocks, 0, FIRST)
    _, near_mine, columns, counts = lax.optimization_barrier(
        (packed, near_mine, columns, counts)
    )
    nears = [near_mine] + [
        lax.ppermute(near_mine, "layer", [(x, (x + d) % layers) for x in range(layers)])
        for d in range(1, layers)
    ]
    outer = lax.ppermute(packed, ("row", "col"), outer_pairs)

    code = jnp.where(get, (4 << 10) + get_pos, 0)
    code = jnp.where(even, code.reshape(rows, slots)[::-1], code.reshape(rows, slots))
    row_at = jnp.arange(rows, dtype=jnp.int32)[:, None] - jnp.where(even, rows - NEAR_ROWS, 0)
    sent = (row_at >= 0) & (row_at < NEAR_ROWS) & (slot_ids < NEAR_SLOTS)
    sent_at = (slot_ids // share * NEAR_ROWS + row_at) * share + slot_ids % share
    far_live = jnp.where(even, live[0], live[2])
    code = jnp.where(sent & far_live, (2 << 10) + sent_at, code)
    ids = ids.reshape(rows, slots)
    own = jnp.where(live[1], (1 << 10) + ids, 0)
    near = jnp.where(even, live[2], live[0])
    near = jnp.where(near, (1 << 10) + span + ids, 0)
    codes = jnp.concatenate(
        [jnp.where(even, code, near), own, jnp.where(even, near, code)], axis=0
    )
    off3 = off.reshape(3 * rows, slots)
    at = lax.broadcasted_iota(jnp.int32, (1, 1, STRIDE), 2)
    table = jnp.sum(
        jnp.where(off3[:, :, None] + BAND == at, codes[:, :, None], 0), axis=1
    ).reshape(-1)
    table = jnp.concatenate([table, jnp.zeros((STRIDE,), jnp.int32)])
    place = jnp.where(
        live[1], jnp.arange(rows, dtype=jnp.int32)[:, None] + off[1], 3 * rows
    ).reshape(-1)
    more = most_needed(columns, counts, layers) > FIRST

    def second():
        late = pack(send_idx, blocks, FIRST, BOUND - FIRST)
        return lax.ppermute(late, ("row", "col"), outer_pairs)

    late = lax.cond(
        more, second, lambda: blank((BOUND - FIRST, edge, edge), values.dtype)
    )
    start = jnp.full((8,), start_slot, jnp.int32)

    acc, held, near_list, far_list, size = local_products(
        start, table, place, blocks, inner, rows, slots, quarter
    )
    acc = near_products(jnp.full((8,), layer, jnp.int32), size, near_list, acc, held, nears)
    more = jnp.full((8,), more, jnp.int32)
    square = far_products(more, size, far_list, acc, held, outer, late, rows, quarter)
    return square.reshape(rows, quarter, edge, edge)


def solution(mesh):
    return jax.shard_map(
        per_device,
        mesh=mesh,
        in_specs=(P(("row", "col"), None, None, None), P(), P()),
        out_specs=P(("row", "col"), "layer", None, None),
        check_vma=False,
    )
```

```python
import functools

import jax
import jax.numpy as jnp
import numpy as np
from jax import lax
from jax.experimental import pallas as pl
from jax.experimental.pallas import tpu as pltpu
from jax.sharding import PartitionSpec as P

BAND = 12
STRIDE = 64
WIDE = 16
UNROLL = 4
NEAR_ROWS = 7
NEAR_SLOTS = 8
FIRST = 68
BOUND = 148
STEP = 5
ANY = pl.BlockSpec(memory_space=pl.ANY)
SMEM = pl.BlockSpec(memory_space=pltpu.SMEM)
VMEM = pl.BlockSpec(memory_space=pltpu.VMEM)


def pack_kernel(start, size, idx_ref, blocks_ref, out_ref, sem):
    def read(p, carry):
        pltpu.make_async_copy(
            blocks_ref.at[idx_ref[start + p]], out_ref.at[p], sem
        ).start()
        return carry

    lax.fori_loop(0, size, read, 0, unroll=4)
    pltpu.make_async_copy(blocks_ref.at[pl.ds(0, size)], out_ref, sem).wait()


def pack(idx, blocks, start, size):
    shape = (size,) + blocks.shape[1:]
    return pl.pallas_call(
        functools.partial(pack_kernel, start, size),
        out_shape=jax.ShapeDtypeStruct(shape, blocks.dtype),
        in_specs=[SMEM, ANY],
        out_specs=VMEM,
        scratch_shapes=[pltpu.SemaphoreType.DMA],
        compiler_params=pltpu.CompilerParams(vmem_limit_bytes=8 << 20),
        name="pack",
    )(idx, blocks)


def run_list(entries, length, a_ref, v_ref, acc_ref):
    def steps(begin, count, carry):
        parts = []
        for u in range(count):
            e0 = entries[(begin + u) * 2]
            e1 = entries[(begin + u) * 2 + 1]
            lhs = jnp.concatenate(
                [a_ref[(e0 >> 10) & 255], a_ref[(e1 >> 10) & 255]], axis=1
            )
            rhs = jnp.concatenate([v_ref[e0 & 1023], v_ref[e1 & 1023]], axis=0)
            parts.append(
                (e0 >> 18, jnp.dot(lhs, rhs, preferred_element_type=jnp.float32))
            )
        for out, part in parts:
            acc_ref[out] += part
        return carry

    pairs = length // 2
    wide = pairs // WIDE
    lax.fori_loop(0, wide, lambda t, c: steps(t * WIDE, WIDE, c), 0)
    rest = (pairs - wide * WIDE) // UNROLL
    lax.fori_loop(0, rest, lambda t, c: steps(wide * WIDE + t * UNROLL, UNROLL, c), 0)


def local_kernel(
    rows,
    slots,
    quarter,
    start_ref,
    table_ref,
    place_ref,
    blocks_ref,
    inner_ref,
    acc_ref,
    a_ref,
    near_ref,
    far_ref,
    size_ref,
    own_ref,
    inner_v,
    sem,
):
    count = rows * slots
    outs = rows * quarter
    size = 2 * UNROLL
    load = pltpu.make_async_copy(inner_ref, inner_v.at[pl.ds(count, count)], sem.at[0])
    load.start()
    load_own = pltpu.make_async_copy(blocks_ref, inner_v.at[pl.ds(0, count)], sem.at[1])
    load_own.start()
    load_a = pltpu.make_async_copy(blocks_ref, a_ref.at[pl.ds(0, count)], sem.at[2])
    load_a.start()
    a_ref[count] = jnp.zeros(a_ref.shape[1:], a_ref.dtype)

    def clear(o, carry):
        acc_ref[o] = jnp.zeros(acc_ref.shape[1:], acc_ref.dtype)
        return carry

    lax.fori_loop(0, outs + 1, clear, 0)
    start_slot = start_ref[0]

    def one_row(i, ends):
        base = i * slots
        row_tag = base << 10
        chunks = (start_ref[1 + i] + STEP - 1) // STEP

        def one_output(p, ends):
            j_at = place_ref[base + start_slot + p]
            tag = row_tag + ((i * quarter + p) << 18)

            def some_terms(c, ends):
                e_own, e_near, e_far = ends
                line = count + base + c * STEP
                some_tag = tag + ((c * STEP) << 10)
                for m in range(STEP):
                    code = table_ref[place_ref[line + m] + (j_at + 2 * BAND)]
                    entry = (code & 1023) + (some_tag + (m << 10))
                    own_ref[e_own] = entry
                    near_ref[e_near] = entry
                    far_ref[e_far] = entry
                    e_own += (code >> 10) & 1
                    e_near += (code >> 11) & 1
                    e_far += code >> 12
                return e_own, e_near, e_far

            def terms(ends):
                e_own, e_near, e_far = lax.fori_loop(0, chunks, some_terms, ends)
                none = ((i * quarter + p) << 18) | (count << 10)
                own_ref[e_own] = none
                near_ref[e_near] = none
                far_ref[e_far] = none
                return e_own + (e_own & 1), e_near + (e_near & 1), e_far + (e_far & 1)

            return lax.cond(j_at < 3 * rows, terms, lambda ends: ends, ends)

        return lax.fori_loop(0, quarter, one_output, ends)

    zero = jnp.int32(0)
    e_own, e_near, e_far = lax.fori_loop(0, rows, one_row, (zero, zero, zero))
    for u in range(size):
        none = (outs << 18) | (count << 10)
        own_ref[e_own + u] = none
        near_ref[e_near + u] = none
        far_ref[e_far + u] = none
    size_ref[0] = (e_near + size - 1) // size * size
    size_ref[1] = (e_far + size - 1) // size * size
    load_own.wait()
    load_a.wait()
    load.wait()
    run_list(own_ref, (e_own + size - 1) // size * size, a_ref, inner_v, acc_ref)


def local_products(start, table, place, blocks, inner, rows, slots, quarter):
    edge = blocks.shape[-1]
    outs = rows * quarter
    length = outs * slots + 4 * UNROLL
    return pl.pallas_call(
        functools.partial(local_kernel, rows, slots, quarter),
        out_shape=(
            jax.ShapeDtypeStruct((outs + 1, edge, edge), jnp.float32),
            jax.ShapeDtypeStruct((rows * slots + 1, edge, edge), blocks.dtype),
            jax.ShapeDtypeStruct((length,), jnp.int32),
            jax.ShapeDtypeStruct((length,), jnp.int32),
            jax.ShapeDtypeStruct((8,), jnp.int32),
        ),
        in_specs=[SMEM, SMEM, SMEM, ANY, ANY],
        out_specs=(VMEM, VMEM, SMEM, SMEM, SMEM),
        scratch_shapes=[
            pltpu.SMEM((length,), jnp.int32),
            pltpu.VMEM((2 * rows * slots, edge, edge), blocks.dtype),
            pltpu.SemaphoreType.DMA((3,)),
        ],
        compiler_params=pltpu.CompilerParams(vmem_limit_bytes=32 << 20),
        cost_estimate=pl.CostEstimate(
            flops=2 * 10**9, bytes_accessed=8 * 10**6, transcendentals=0
        ),
        name="local_products",
    )(start, table, place, blocks, inner)


def near_kernel(
    layer_ref,
    size_ref,
    list_ref,
    acc_in,
    a_ref,
    near0_ref,
    near1_ref,
    near2_ref,
    near3_ref,
    acc_ref,
    v_ref,
    sem,
):
    nears = (near0_ref, near1_ref, near2_ref, near3_ref)
    near = near0_ref.shape[0]
    copies = []
    for away, ref in enumerate(nears):
        source = lax.rem(layer_ref[0] + len(nears) - away, len(nears))
        copies.append(
            pltpu.make_async_copy(
                ref, v_ref.at[pl.ds(source * near, near)], sem.at[away]
            )
        )
    for copy in copies:
        copy.start()
    for copy in copies:
        copy.wait()
    run_list(list_ref, size_ref[0], a_ref, v_ref, acc_ref)


def near_products(layer, size, entries, acc, blocks, nears):
    edge = blocks.shape[-1]
    held = len(nears) * nears[0].shape[0]
    return pl.pallas_call(
        near_kernel,
        out_shape=jax.ShapeDtypeStruct(acc.shape, acc.dtype),
        in_specs=[SMEM] * 3 + [VMEM, VMEM] + [ANY] * len(nears),
        out_specs=VMEM,
        scratch_shapes=[
            pltpu.VMEM((held, edge, edge), blocks.dtype),
            pltpu.SemaphoreType.DMA((len(nears),)),
        ],
        input_output_aliases={3: 0},
        compiler_params=pltpu.CompilerParams(vmem_limit_bytes=24 << 20),
        name="near_products",
    )(layer, size, entries, acc, blocks, *nears)


def far_kernel(
    rows,
    quarter,
    more_ref,
    size_ref,
    list_ref,
    acc_in,
    a_ref,
    first_ref,
    late_ref,
    out_ref,
    acc_ref,
    v_ref,
    held,
    sem,
):
    first, late = first_ref.shape[0], late_ref.shape[0]

    @pl.when(more_ref[0] == 0)
    def _():
        run_list(list_ref, size_ref[1], a_ref, first_ref, acc_ref)

    @pl.when(more_ref[0] != 0)
    def _():
        late_copy = pltpu.make_async_copy(
            late_ref, v_ref.at[pl.ds(first, late)], sem.at[0]
        )
        late_copy.start()

        def move(b, carry):
            v_ref[b] = first_ref[b]
            return carry

        lax.fori_loop(0, first, move, 0)
        late_copy.wait()
        run_list(list_ref, size_ref[1], a_ref, v_ref, acc_ref)

    def finish(i, carry):
        part = pl.ds(i * quarter, quarter)
        held[part] = acc_ref[part].astype(held.dtype)
        pltpu.make_async_copy(held.at[part], out_ref.at[part], sem.at[1]).start()
        return carry

    lax.fori_loop(0, rows, finish, 0)
    pltpu.make_async_copy(held, out_ref, sem.at[1]).wait()


def far_products(more, size, entries, acc, blocks, first, late, rows, quarter):
    edge = blocks.shape[-1]
    outs = rows * quarter
    held = first.shape[0] + late.shape[0]
    square, _ = pl.pallas_call(
        functools.partial(far_kernel, rows, quarter),
        out_shape=(
            jax.ShapeDtypeStruct((outs, edge, edge), blocks.dtype),
            jax.ShapeDtypeStruct(acc.shape, acc.dtype),
        ),
        in_specs=[SMEM] * 3 + [VMEM, VMEM, VMEM, ANY],
        out_specs=(ANY, VMEM),
        scratch_shapes=[
            pltpu.VMEM((held, edge, edge), blocks.dtype),
            pltpu.VMEM((outs, edge, edge), blocks.dtype),
            pltpu.SemaphoreType.DMA((2,)),
        ],
        input_output_aliases={3: 1},
        compiler_params=pltpu.CompilerParams(vmem_limit_bytes=24 << 20),
        name="far_products",
    )(more, size, entries, acc, blocks, first, late)
    return square


def blank(shape, dtype):
    return pl.pallas_call(
        lambda out_ref: None,
        out_shape=jax.ShapeDtypeStruct(shape, dtype),
        out_specs=ANY,
        name="blank",
    )()


def or_reduce(x, axis):
    return lax.reduce(x, jnp.uint32(0), lax.bitwise_or, (axis,))


def bit_masks(off, live):
    bits = jnp.where(live, jnp.uint32(1) << off.astype(jnp.uint32), jnp.uint32(0))
    return or_reduce(bits, 1), bits


def needed(k_mask, i_mask, i_part, later):
    rows = k_mask.shape[-1]
    kk = lax.broadcasted_iota(jnp.int32, (rows, rows), 0)
    ii = lax.broadcasted_iota(jnp.int32, (rows, rows), 1)
    ahead = ii - kk if later else kk - ii
    valid = ahead <= 0
    shift = jnp.where(valid, rows + ahead, 0).astype(jnp.uint32)
    at = BAND - shift if later else BAND + shift
    has = valid & (((i_mask[..., None, :] >> at) & 1) == 1)
    moved = i_part[..., None, :] << shift if later else i_part[..., None, :] >> shift
    return k_mask & or_reduce(jnp.where(has, moved, jnp.uint32(0)), moved.ndim - 1)


def most_needed(columns, counts, layers):
    total_rows, slots = columns.shape
    quarter = slots // layers
    rows_id = jnp.arange(total_rows, dtype=jnp.int32)
    off = (columns - rows_id[:, None] + BAND) % total_rows
    slot_ids = jnp.arange(slots, dtype=jnp.int32)
    live = slot_ids[None, :] < counts[:, None]
    mask, bits = bit_masks(off, live)
    part = jnp.stack(
        [or_reduce(bits[:, q * quarter : (q + 1) * quarter], 1) for q in range(layers)]
    )
    mask_wrap = jnp.concatenate([mask[-BAND:], mask, mask[:BAND]])
    part_wrap = jnp.concatenate([part[:, -BAND:], part, part[:, :BAND]], axis=1)
    kk = rows_id % BAND
    up = jnp.zeros_like(part)
    down = jnp.zeros_like(part)
    for s in range(1, BAND + 1):
        i_mask = mask_wrap[BAND + s : BAND + s + total_rows]
        i_part = part_wrap[:, BAND + s : BAND + s + total_rows]
        has = (((i_mask >> (BAND - s)) & 1) == 1) & (kk + s >= BAND)
        up = up | jnp.where(has, i_part << s, jnp.uint32(0))
        i_mask = mask_wrap[BAND - s : BAND - s + total_rows]
        i_part = part_wrap[:, BAND - s : BAND - s + total_rows]
        has = (((i_mask >> (BAND + s)) & 1) == 1) & (kk - s < 0)
        down = down | jnp.where(has, i_part >> s, jnp.uint32(0))
    odd = (rows_id // BAND) % 2 == 1
    fixed = or_reduce(bits[:, :NEAR_SLOTS], 1)
    close = jnp.where(odd, kk >= BAND - NEAR_ROWS, kk < NEAR_ROWS)
    asked = jnp.where(odd, up, down) & mask & jnp.where(close, ~fixed, ~jnp.uint32(0))
    per_row = lax.population_count(asked).astype(jnp.bfloat16)
    member = np.arange(total_rows)[:, None] // BAND == np.arange(total_rows // BAND)
    per_group = jnp.dot(
        per_row, jnp.asarray(member, jnp.bfloat16), preferred_element_type=jnp.float32
    )
    return jnp.max(per_group)


def per_device(values, columns, counts):
    rows, slots, edge, _ = values.shape
    layers = lax.axis_size("layer")
    quarter = slots // layers
    start_slot = lax.axis_index("layer") * quarter
    total_rows = columns.shape[0]
    group = lax.axis_index(("row", "col"))
    groups = lax.axis_size(("row", "col"))
    even = group % 2 == 0
    first_row = group * rows
    blocks = values.reshape((-1, edge, edge))
    span = rows * slots

    inner = lax.ppermute(blocks, ("row", "col"), [(g, g ^ 1) for g in range(groups)])

    share = NEAR_SLOTS // layers
    layer = lax.axis_index("layer")
    outer_pairs = [
        (g, (g - 1) % groups if g % 2 == 0 else (g + 1) % groups) for g in range(groups)
    ]
    near_rows = lax.dynamic_slice(
        values,
        (jnp.where(even, 0, rows - NEAR_ROWS), layer * share, 0, 0),
        (NEAR_ROWS, share, edge, edge),
    ).reshape(-1, edge, edge)
    near_mine = lax.ppermute(near_rows, ("row", "col"), outer_pairs)
    both = jnp.concatenate([columns.T, counts[None, :]], axis=0)
    both = lax.optimization_barrier(both)
    both = jnp.concatenate([both[:, -rows:], both, both[:, :rows]], axis=1)
    both = lax.dynamic_slice_in_dim(both, first_row, 3 * rows, 1)
    cols, cnts = both[:slots].T, both[slots]
    row_ids = first_row - rows + jnp.arange(3 * rows, dtype=jnp.int32)
    off = (cols - row_ids[:, None] + BAND) % total_rows
    slot_ids = jnp.arange(slots, dtype=jnp.int32)[None, :]
    live = slot_ids < cnts[:, None]
    mask, bits = bit_masks(off, live)
    mine = (slot_ids >= start_slot) & (slot_ids < start_slot + quarter)
    part = or_reduce(jnp.where(mine, bits, jnp.uint32(0)), 1)
    mask = mask.reshape(3, rows)
    part = part.reshape(3, rows)
    off = off.reshape(3, rows, slots)
    live = live.reshape(3, rows, slots)

    def pair(x):
        return jnp.where(even, x[:2], x[1:])

    mask2, part2, off2, live2 = pair(mask), pair(part), pair(off), pair(live)
    ask = jnp.stack(
        [
            needed(mask2[0], mask2[1], part2[1], True),
            needed(mask2[1], mask2[0], part2[0], False),
        ]
    )
    need = (((ask[:, :, None] >> off2.astype(jnp.uint32)) & 1) == 1) & live2
    fixed = (jnp.arange(rows)[:, None] < NEAR_ROWS) & (slot_ids < NEAR_SLOTS)
    need = jnp.stack([need[0, ::-1], need[1]]) & ~fixed
    need = need.reshape(2, span)
    before = (
        lax.broadcasted_iota(jnp.int32, (span, span), 0)
        < lax.broadcasted_iota(jnp.int32, (span, span), 1)
    ).astype(jnp.bfloat16)
    pos = jnp.dot(
        need.astype(jnp.bfloat16), before, preferred_element_type=jnp.float32
    ).astype(jnp.int32)
    ids = jnp.arange(span, dtype=jnp.int32)
    ids_up = (rows - 1 - ids // slots) * slots + ids % slots
    give, give_pos = jnp.where(even, need[1], need[0]), jnp.where(even, pos[1], pos[0])
    give_ids = jnp.where(even, ids, ids_up)
    get, get_pos = jnp.where(even, need[0], need[1]), jnp.where(even, pos[0], pos[1])
    hit = give[:, None] & (
        give_pos[:, None] == jnp.arange(BOUND, dtype=jnp.int32)[None, :]
    )
    send_idx = jnp.sum(jnp.where(hit, give_ids[:, None], 0), axis=0)

    packed = pack(send_idx, blocks, 0, FIRST)
    _, near_mine, columns, counts = lax.optimization_barrier(
        (packed, near_mine, columns, counts)
    )
    nears = [near_mine] + [
        lax.ppermute(near_mine, "layer", [(x, (x + d) % layers) for x in range(layers)])
        for d in range(1, layers)
    ]
    outer = lax.ppermute(packed, ("row", "col"), outer_pairs)

    code = jnp.where(get, (4 << 10) + get_pos, 0)
    code = jnp.where(even, code.reshape(rows, slots)[::-1], code.reshape(rows, slots))
    row_at = jnp.arange(rows, dtype=jnp.int32)[:, None] - jnp.where(even, rows - NEAR_ROWS, 0)
    sent = (row_at >= 0) & (row_at < NEAR_ROWS) & (slot_ids < NEAR_SLOTS)
    sent_at = (slot_ids // share * NEAR_ROWS + row_at) * share + slot_ids % share
    far_live = jnp.where(even, live[0], live[2])
    code = jnp.where(sent & far_live, (2 << 10) + sent_at, code)
    ids = ids.reshape(rows, slots)
    own = jnp.where(live[1], (1 << 10) + ids, 0)
    near = jnp.where(even, live[2], live[0])
    near = jnp.where(near, (1 << 10) + span + ids, 0)
    codes = jnp.concatenate(
        [jnp.where(even, code, near), own, jnp.where(even, near, code)], axis=0
    )
    off3 = off.reshape(3 * rows, slots)
    at = lax.broadcasted_iota(jnp.int32, (1, 1, STRIDE), 2)
    table = jnp.sum(
        jnp.where(off3[:, :, None] + BAND == at, codes[:, :, None], 0), axis=1
    ).reshape(-1)
    table = jnp.concatenate([table, jnp.zeros((STRIDE,), jnp.int32)])
    place = jnp.where(
        live[1], jnp.arange(rows, dtype=jnp.int32)[:, None] + off[1], 3 * rows
    ).reshape(-1)
    inner, columns, counts = lax.optimization_barrier((inner, columns, counts))
    more = most_needed(columns, counts, layers) > FIRST

    def second():
        late = pack(send_idx, blocks, FIRST, BOUND - FIRST)
        return lax.ppermute(late, ("row", "col"), outer_pairs)

    late = lax.cond(
        more, second, lambda: blank((BOUND - FIRST, edge, edge), values.dtype)
    )
    place = jnp.concatenate([place, place * (STRIDE - 1)])
    start = jnp.concatenate([start_slot[None], cnts[rows : 2 * rows]]).astype(jnp.int32)

    acc, held, near_list, far_list, size = local_products(
        start, table, place, blocks, inner, rows, slots, quarter
    )
    acc = near_products(jnp.full((8,), layer, jnp.int32), size, near_list, acc, held, nears)
    more = jnp.full((8,), more, jnp.int32)
    square = far_products(more, size, far_list, acc, held, outer, late, rows, quarter)
    return square.reshape(rows, quarter, edge, edge)


def solution(mesh):
    return jax.shard_map(
        per_device,
        mesh=mesh,
        in_specs=(P(("row", "col"), None, None, None), P(), P()),
        out_specs=P(("row", "col"), "layer", None, None),
        check_vma=False,
    )
```

```python
import functools

import jax
import jax.numpy as jnp
import numpy as np
from jax import lax
from jax.experimental import pallas as pl
from jax.experimental.pallas import tpu as pltpu
from jax.sharding import PartitionSpec as P

BAND = 12
STRIDE = 64
WIDE = 16
UNROLL = 4
NEAR_ROWS = 5
NEAR_SLOTS = 12
FIRST = 68
BOUND = 140
ANY = pl.BlockSpec(memory_space=pl.ANY)
SMEM = pl.BlockSpec(memory_space=pltpu.SMEM)
VMEM = pl.BlockSpec(memory_space=pltpu.VMEM)


def pack_kernel(start, size, idx_ref, blocks_ref, out_ref, sem):
    def read(p, carry):
        pltpu.make_async_copy(
            blocks_ref.at[idx_ref[start + p]], out_ref.at[p], sem
        ).start()
        return carry

    lax.fori_loop(0, size, read, 0, unroll=4)
    pltpu.make_async_copy(blocks_ref.at[pl.ds(0, size)], out_ref, sem).wait()


def pack(idx, blocks, start, size):
    shape = (size,) + blocks.shape[1:]
    return pl.pallas_call(
        functools.partial(pack_kernel, start, size),
        out_shape=jax.ShapeDtypeStruct(shape, blocks.dtype),
        in_specs=[SMEM, ANY],
        out_specs=VMEM,
        scratch_shapes=[pltpu.SemaphoreType.DMA],
        compiler_params=pltpu.CompilerParams(vmem_limit_bytes=8 << 20),
        name="pack",
    )(idx, blocks)


def run_list(entries, length, a_ref, v_ref, acc_ref):
    def steps(begin, count, carry):
        parts = []
        for u in range(count):
            e0 = entries[(begin + u) * 2]
            e1 = entries[(begin + u) * 2 + 1]
            lhs = jnp.concatenate(
                [a_ref[(e0 >> 10) & 255], a_ref[(e1 >> 10) & 255]], axis=1
            )
            rhs = jnp.concatenate([v_ref[e0 & 1023], v_ref[e1 & 1023]], axis=0)
            parts.append(
                (e0 >> 18, jnp.dot(lhs, rhs, preferred_element_type=jnp.float32))
            )
        for out, part in parts:
            acc_ref[out] += part
        return carry

    pairs = length // 2
    wide = pairs // WIDE
    lax.fori_loop(0, wide, lambda t, c: steps(t * WIDE, WIDE, c), 0)
    rest = (pairs - wide * WIDE) // UNROLL
    lax.fori_loop(0, rest, lambda t, c: steps(wide * WIDE + t * UNROLL, UNROLL, c), 0)


def local_kernel(
    rows,
    slots,
    quarter,
    start_ref,
    table_ref,
    place_ref,
    blocks_ref,
    inner_ref,
    acc_ref,
    a_ref,
    near_ref,
    far_ref,
    size_ref,
    own_ref,
    inner_v,
    sem,
):
    count = rows * slots
    outs = rows * quarter
    size = 2 * UNROLL
    load = pltpu.make_async_copy(inner_ref, inner_v.at[pl.ds(count, count)], sem.at[0])
    load.start()
    load_own = pltpu.make_async_copy(blocks_ref, inner_v.at[pl.ds(0, count)], sem.at[1])
    load_own.start()
    load_a = pltpu.make_async_copy(blocks_ref, a_ref.at[pl.ds(0, count)], sem.at[2])
    load_a.start()
    a_ref[count] = jnp.zeros(a_ref.shape[1:], a_ref.dtype)

    def clear(o, carry):
        acc_ref[o] = jnp.zeros(acc_ref.shape[1:], acc_ref.dtype)
        return carry

    lax.fori_loop(0, outs + 1, clear, 0)
    start_slot = start_ref[0]

    def one_row(i, ends):
        base = i * slots
        row_tag = base << 10
        terms_at = [place_ref[base + m] * (STRIDE - 1) for m in range(slots)]

        def one_output(p, ends):
            j_at = place_ref[base + start_slot + p]
            tag = row_tag + ((i * quarter + p) << 18)

            def terms(ends):
                e_own, e_near, e_far = ends
                for m in range(slots):
                    code = table_ref[terms_at[m] + (j_at + 2 * BAND)]
                    entry = (code & 1023) + (tag + (m << 10))
                    own_ref[e_own] = entry
                    near_ref[e_near] = entry
                    far_ref[e_far] = entry
                    e_own += (code >> 10) & 1
                    e_near += (code >> 11) & 1
                    e_far += code >> 12
                none = ((i * quarter + p) << 18) | (count << 10)
                own_ref[e_own] = none
                near_ref[e_near] = none
                far_ref[e_far] = none
                return e_own + (e_own & 1), e_near + (e_near & 1), e_far + (e_far & 1)

            return lax.cond(j_at < 3 * rows, terms, lambda ends: ends, ends)

        return lax.fori_loop(0, quarter, one_output, ends)

    zero = jnp.int32(0)
    e_own, e_near, e_far = lax.fori_loop(0, rows, one_row, (zero, zero, zero))
    for u in range(size):
        none = (outs << 18) | (count << 10)
        own_ref[e_own + u] = none
        near_ref[e_near + u] = none
        far_ref[e_far + u] = none
    size_ref[0] = (e_near + size - 1) // size * size
    size_ref[1] = (e_far + size - 1) // size * size
    load_own.wait()
    load_a.wait()
    load.wait()
    run_list(own_ref, (e_own + size - 1) // size * size, a_ref, inner_v, acc_ref)


def local_products(start, table, place, blocks, inner, rows, slots, quarter):
    edge = blocks.shape[-1]
    outs = rows * quarter
    length = outs * slots + 4 * UNROLL
    return pl.pallas_call(
        functools.partial(local_kernel, rows, slots, quarter),
        out_shape=(
            jax.ShapeDtypeStruct((outs + 1, edge, edge), jnp.float32),
            jax.ShapeDtypeStruct((rows * slots + 1, edge, edge), blocks.dtype),
            jax.ShapeDtypeStruct((length,), jnp.int32),
            jax.ShapeDtypeStruct((length,), jnp.int32),
            jax.ShapeDtypeStruct((8,), jnp.int32),
        ),
        in_specs=[SMEM, SMEM, SMEM, ANY, ANY],
        out_specs=(VMEM, VMEM, SMEM, SMEM, SMEM),
        scratch_shapes=[
            pltpu.SMEM((length,), jnp.int32),
            pltpu.VMEM((2 * rows * slots, edge, edge), blocks.dtype),
            pltpu.SemaphoreType.DMA((3,)),
        ],
        compiler_params=pltpu.CompilerParams(vmem_limit_bytes=32 << 20),
        cost_estimate=pl.CostEstimate(
            flops=2 * 10**9, bytes_accessed=8 * 10**6, transcendentals=0
        ),
        name="local_products",
    )(start, table, place, blocks, inner)


def near_kernel(
    layer_ref,
    size_ref,
    list_ref,
    acc_in,
    a_ref,
    near0_ref,
    near1_ref,
    near2_ref,
    near3_ref,
    acc_ref,
    v_ref,
    sem,
):
    nears = (near0_ref, near1_ref, near2_ref, near3_ref)
    near = near0_ref.shape[0]
    copies = []
    for away, ref in enumerate(nears):
        source = lax.rem(layer_ref[0] + len(nears) - away, len(nears))
        copies.append(
            pltpu.make_async_copy(
                ref, v_ref.at[pl.ds(source * near, near)], sem.at[away]
            )
        )
    for copy in copies:
        copy.start()
    for copy in copies:
        copy.wait()
    run_list(list_ref, size_ref[0], a_ref, v_ref, acc_ref)


def near_products(layer, size, entries, acc, blocks, nears):
    edge = blocks.shape[-1]
    held = len(nears) * nears[0].shape[0]
    return pl.pallas_call(
        near_kernel,
        out_shape=jax.ShapeDtypeStruct(acc.shape, acc.dtype),
        in_specs=[SMEM] * 3 + [VMEM, VMEM] + [ANY] * len(nears),
        out_specs=VMEM,
        scratch_shapes=[
            pltpu.VMEM((held, edge, edge), blocks.dtype),
            pltpu.SemaphoreType.DMA((len(nears),)),
        ],
        input_output_aliases={3: 0},
        compiler_params=pltpu.CompilerParams(vmem_limit_bytes=24 << 20),
        name="near_products",
    )(layer, size, entries, acc, blocks, *nears)


def far_kernel(
    rows,
    quarter,
    more_ref,
    size_ref,
    list_ref,
    acc_in,
    a_ref,
    first_ref,
    late_ref,
    out_ref,
    acc_ref,
    v_ref,
    held,
    sem,
):
    first, late = first_ref.shape[0], late_ref.shape[0]

    @pl.when(more_ref[0] == 0)
    def _():
        run_list(list_ref, size_ref[1], a_ref, first_ref, acc_ref)

    @pl.when(more_ref[0] != 0)
    def _():
        late_copy = pltpu.make_async_copy(
            late_ref, v_ref.at[pl.ds(first, late)], sem.at[0]
        )
        late_copy.start()

        def move(b, carry):
            v_ref[b] = first_ref[b]
            return carry

        lax.fori_loop(0, first, move, 0)
        late_copy.wait()
        run_list(list_ref, size_ref[1], a_ref, v_ref, acc_ref)

    def finish(i, carry):
        part = pl.ds(i * quarter, quarter)
        held[part] = acc_ref[part].astype(held.dtype)
        pltpu.make_async_copy(held.at[part], out_ref.at[part], sem.at[1]).start()
        return carry

    lax.fori_loop(0, rows, finish, 0)
    pltpu.make_async_copy(held, out_ref, sem.at[1]).wait()


def far_products(more, size, entries, acc, blocks, first, late, rows, quarter):
    edge = blocks.shape[-1]
    outs = rows * quarter
    held = first.shape[0] + late.shape[0]
    square, _ = pl.pallas_call(
        functools.partial(far_kernel, rows, quarter),
        out_shape=(
            jax.ShapeDtypeStruct((outs, edge, edge), blocks.dtype),
            jax.ShapeDtypeStruct(acc.shape, acc.dtype),
        ),
        in_specs=[SMEM] * 3 + [VMEM, VMEM, VMEM, ANY],
        out_specs=(ANY, VMEM),
        scratch_shapes=[
            pltpu.VMEM((held, edge, edge), blocks.dtype),
            pltpu.VMEM((outs, edge, edge), blocks.dtype),
            pltpu.SemaphoreType.DMA((2,)),
        ],
        input_output_aliases={3: 1},
        compiler_params=pltpu.CompilerParams(vmem_limit_bytes=24 << 20),
        name="far_products",
    )(more, size, entries, acc, blocks, first, late)
    return square


def blank(shape, dtype):
    return pl.pallas_call(
        lambda out_ref: None,
        out_shape=jax.ShapeDtypeStruct(shape, dtype),
        out_specs=ANY,
        name="blank",
    )()


def or_reduce(x, axis):
    return lax.reduce(x, jnp.uint32(0), lax.bitwise_or, (axis,))


def bit_masks(off, live):
    bits = jnp.where(live, jnp.uint32(1) << off.astype(jnp.uint32), jnp.uint32(0))
    return or_reduce(bits, 1), bits


def needed(k_mask, i_mask, i_part, later):
    rows = k_mask.shape[-1]
    kk = lax.broadcasted_iota(jnp.int32, (rows, rows), 0)
    ii = lax.broadcasted_iota(jnp.int32, (rows, rows), 1)
    ahead = ii - kk if later else kk - ii
    valid = ahead <= 0
    shift = jnp.where(valid, rows + ahead, 0).astype(jnp.uint32)
    at = BAND - shift if later else BAND + shift
    has = valid & (((i_mask[..., None, :] >> at) & 1) == 1)
    moved = i_part[..., None, :] << shift if later else i_part[..., None, :] >> shift
    return k_mask & or_reduce(jnp.where(has, moved, jnp.uint32(0)), moved.ndim - 1)


def most_needed(columns, counts, layers):
    total_rows, slots = columns.shape
    quarter = slots // layers
    rows_id = jnp.arange(total_rows, dtype=jnp.int32)
    off = (columns - rows_id[:, None] + BAND) % total_rows
    slot_ids = jnp.arange(slots, dtype=jnp.int32)
    live = slot_ids[None, :] < counts[:, None]
    mask, bits = bit_masks(off, live)
    part = jnp.stack(
        [or_reduce(bits[:, q * quarter : (q + 1) * quarter], 1) for q in range(layers)]
    )
    mask_wrap = jnp.concatenate([mask[-BAND:], mask, mask[:BAND]])
    part_wrap = jnp.concatenate([part[:, -BAND:], part, part[:, :BAND]], axis=1)
    kk = rows_id % BAND
    up = jnp.zeros_like(part)
    down = jnp.zeros_like(part)
    for s in range(1, BAND + 1):
        i_mask = mask_wrap[BAND + s : BAND + s + total_rows]
        i_part = part_wrap[:, BAND + s : BAND + s + total_rows]
        has = (((i_mask >> (BAND - s)) & 1) == 1) & (kk + s >= BAND)
        up = up | jnp.where(has, i_part << s, jnp.uint32(0))
        i_mask = mask_wrap[BAND - s : BAND - s + total_rows]
        i_part = part_wrap[:, BAND - s : BAND - s + total_rows]
        has = (((i_mask >> (BAND + s)) & 1) == 1) & (kk - s < 0)
        down = down | jnp.where(has, i_part >> s, jnp.uint32(0))
    odd = (rows_id // BAND) % 2 == 1
    fixed = or_reduce(bits[:, :NEAR_SLOTS], 1)
    close = jnp.where(odd, kk >= BAND - NEAR_ROWS, kk < NEAR_ROWS)
    asked = jnp.where(odd, up, down) & mask & jnp.where(close, ~fixed, ~jnp.uint32(0))
    per_row = lax.population_count(asked).astype(jnp.bfloat16)
    member = np.arange(total_rows)[:, None] // BAND == np.arange(total_rows // BAND)
    per_group = jnp.dot(
        per_row, jnp.asarray(member, jnp.bfloat16), preferred_element_type=jnp.float32
    )
    return jnp.max(per_group)


def per_device(values, columns, counts):
    rows, slots, edge, _ = values.shape
    layers = lax.axis_size("layer")
    quarter = slots // layers
    start_slot = lax.axis_index("layer") * quarter
    total_rows = columns.shape[0]
    group = lax.axis_index(("row", "col"))
    groups = lax.axis_size(("row", "col"))
    even = group % 2 == 0
    first_row = group * rows
    blocks = values.reshape((-1, edge, edge))
    span = rows * slots

    inner = lax.ppermute(blocks, ("row", "col"), [(g, g ^ 1) for g in range(groups)])

    share = NEAR_SLOTS // layers
    layer = lax.axis_index("layer")
    outer_pairs = [
        (g, (g - 1) % groups if g % 2 == 0 else (g + 1) % groups) for g in range(groups)
    ]
    near_rows = lax.dynamic_slice(
        values,
        (jnp.where(even, 0, rows - NEAR_ROWS), layer * share, 0, 0),
        (NEAR_ROWS, share, edge, edge),
    ).reshape(-1, edge, edge)
    near_mine = lax.ppermute(near_rows, ("row", "col"), outer_pairs)
    both = jnp.concatenate([columns.T, counts[None, :]], axis=0)
    both = lax.optimization_barrier(both)
    both = jnp.concatenate([both[:, -rows:], both, both[:, :rows]], axis=1)
    both = lax.dynamic_slice_in_dim(both, first_row, 3 * rows, 1)
    cols, cnts = both[:slots].T, both[slots]
    row_ids = first_row - rows + jnp.arange(3 * rows, dtype=jnp.int32)
    off = (cols - row_ids[:, None] + BAND) % total_rows
    slot_ids = jnp.arange(slots, dtype=jnp.int32)[None, :]
    live = slot_ids < cnts[:, None]
    mask, bits = bit_masks(off, live)
    mine = (slot_ids >= start_slot) & (slot_ids < start_slot + quarter)
    part = or_reduce(jnp.where(mine, bits, jnp.uint32(0)), 1)
    mask = mask.reshape(3, rows)
    part = part.reshape(3, rows)
    off = off.reshape(3, rows, slots)
    live = live.reshape(3, rows, slots)

    def pair(x):
        return jnp.where(even, x[:2], x[1:])

    mask2, part2, off2, live2 = pair(mask), pair(part), pair(off), pair(live)
    ask = jnp.stack(
        [
            needed(mask2[0], mask2[1], part2[1], True),
            needed(mask2[1], mask2[0], part2[0], False),
        ]
    )
    need = (((ask[:, :, None] >> off2.astype(jnp.uint32)) & 1) == 1) & live2
    fixed = (jnp.arange(rows)[:, None] < NEAR_ROWS) & (slot_ids < NEAR_SLOTS)
    need = jnp.stack([need[0, ::-1], need[1]]) & ~fixed
    need = need.reshape(2, span)
    before = (
        lax.broadcasted_iota(jnp.int32, (span, span), 0)
        < lax.broadcasted_iota(jnp.int32, (span, span), 1)
    ).astype(jnp.bfloat16)
    pos = jnp.dot(
        need.astype(jnp.bfloat16), before, preferred_element_type=jnp.float32
    ).astype(jnp.int32)
    ids = jnp.arange(span, dtype=jnp.int32)
    ids_up = (rows - 1 - ids // slots) * slots + ids % slots
    give, give_pos = jnp.where(even, need[1], need[0]), jnp.where(even, pos[1], pos[0])
    give_ids = jnp.where(even, ids, ids_up)
    get, get_pos = jnp.where(even, need[0], need[1]), jnp.where(even, pos[0], pos[1])
    hit = give[:, None] & (
        give_pos[:, None] == jnp.arange(BOUND, dtype=jnp.int32)[None, :]
    )
    send_idx = jnp.sum(jnp.where(hit, give_ids[:, None], 0), axis=0)

    packed = pack(send_idx, blocks, 0, FIRST)
    _, near_mine, columns, counts = lax.optimization_barrier(
        (packed, near_mine, columns, counts)
    )
    nears = [near_mine] + [
        lax.ppermute(near_mine, "layer", [(x, (x + d) % layers) for x in range(layers)])
        for d in range(1, layers)
    ]
    outer = lax.ppermute(packed, ("row", "col"), outer_pairs)

    code = jnp.where(get, (4 << 10) + get_pos, 0)
    code = jnp.where(even, code.reshape(rows, slots)[::-1], code.reshape(rows, slots))
    row_at = jnp.arange(rows, dtype=jnp.int32)[:, None] - jnp.where(even, rows - NEAR_ROWS, 0)
    sent = (row_at >= 0) & (row_at < NEAR_ROWS) & (slot_ids < NEAR_SLOTS)
    sent_at = (slot_ids // share * NEAR_ROWS + row_at) * share + slot_ids % share
    far_live = jnp.where(even, live[0], live[2])
    code = jnp.where(sent & far_live, (2 << 10) + sent_at, code)
    ids = ids.reshape(rows, slots)
    own = jnp.where(live[1], (1 << 10) + ids, 0)
    near = jnp.where(even, live[2], live[0])
    near = jnp.where(near, (1 << 10) + span + ids, 0)
    codes = jnp.concatenate(
        [jnp.where(even, code, near), own, jnp.where(even, near, code)], axis=0
    )
    off3 = off.reshape(3 * rows, slots)
    at = lax.broadcasted_iota(jnp.int32, (1, 1, STRIDE), 2)
    table = jnp.sum(
        jnp.where(off3[:, :, None] + BAND == at, codes[:, :, None], 0), axis=1
    ).reshape(-1)
    table = jnp.concatenate([table, jnp.zeros((STRIDE,), jnp.int32)])
    place = jnp.where(
        live[1], jnp.arange(rows, dtype=jnp.int32)[:, None] + off[1], 3 * rows
    ).reshape(-1)
    inner, columns, counts = lax.optimization_barrier((inner, columns, counts))
    more = most_needed(columns, counts, layers) > FIRST

    def second():
        late = pack(send_idx, blocks, FIRST, BOUND - FIRST)
        return lax.ppermute(late, ("row", "col"), outer_pairs)

    late = lax.cond(
        more, second, lambda: blank((BOUND - FIRST, edge, edge), values.dtype)
    )
    start = jnp.full((8,), start_slot, jnp.int32)

    acc, held, near_list, far_list, size = local_products(
        start, table, place, blocks, inner, rows, slots, quarter
    )
    acc = near_products(jnp.full((8,), layer, jnp.int32), size, near_list, acc, held, nears)
    more = jnp.full((8,), more, jnp.int32)
    square = far_products(more, size, far_list, acc, held, outer, late, rows, quarter)
    return square.reshape(rows, quarter, edge, edge)


def solution(mesh):
    return jax.shard_map(
        per_device,
        mesh=mesh,
        in_specs=(P(("row", "col"), None, None, None), P(), P()),
        out_specs=P(("row", "col"), "layer", None, None),
        check_vma=False,
    )
```

```python
import functools

import jax
import jax.numpy as jnp
import numpy as np
from jax import lax
from jax.experimental import pallas as pl
from jax.experimental.pallas import tpu as pltpu
from jax.sharding import PartitionSpec as P

BAND = 12
STRIDE = 64
WIDE = 16
UNROLL = 4
NEAR_ROWS = 5
NEAR_SLOTS = 12
FIRST = 68
BOUND = 140
ANY = pl.BlockSpec(memory_space=pl.ANY)
SMEM = pl.BlockSpec(memory_space=pltpu.SMEM)
VMEM = pl.BlockSpec(memory_space=pltpu.VMEM)


def pack_kernel(start, size, idx_ref, blocks_ref, out_ref, sem):
    def read(p, carry):
        pltpu.make_async_copy(
            blocks_ref.at[idx_ref[start + p]], out_ref.at[p], sem
        ).start()
        return carry

    lax.fori_loop(0, size, read, 0, unroll=4)
    pltpu.make_async_copy(blocks_ref.at[pl.ds(0, size)], out_ref, sem).wait()


def pack(idx, blocks, start, size):
    shape = (size,) + blocks.shape[1:]
    return pl.pallas_call(
        functools.partial(pack_kernel, start, size),
        out_shape=jax.ShapeDtypeStruct(shape, blocks.dtype),
        in_specs=[SMEM, ANY],
        out_specs=VMEM,
        scratch_shapes=[pltpu.SemaphoreType.DMA],
        compiler_params=pltpu.CompilerParams(vmem_limit_bytes=8 << 20),
        name="pack",
    )(idx, blocks)


def run_list(entries, length, a_ref, v_ref, acc_ref):
    def steps(begin, count, carry):
        parts = []
        for u in range(count):
            e0 = entries[(begin + u) * 2]
            e1 = entries[(begin + u) * 2 + 1]
            lhs = jnp.concatenate(
                [a_ref[(e0 >> 10) & 255], a_ref[(e1 >> 10) & 255]], axis=1
            )
            rhs = jnp.concatenate([v_ref[e0 & 1023], v_ref[e1 & 1023]], axis=0)
            parts.append(
                ((e0 >> 18) & 63, jnp.dot(lhs, rhs, preferred_element_type=jnp.float32))
            )
        for out, part in parts:
            acc_ref[out] += part
        return carry

    pairs = length // 2
    wide = pairs // WIDE
    lax.fori_loop(0, wide, lambda t, c: steps(t * WIDE, WIDE, c), 0)
    rest = (pairs - wide * WIDE) // UNROLL
    lax.fori_loop(0, rest, lambda t, c: steps(wide * WIDE + t * UNROLL, UNROLL, c), 0)


def local_kernel(
    rows,
    slots,
    quarter,
    start_ref,
    table_ref,
    place_ref,
    blocks_ref,
    inner_ref,
    acc_ref,
    a_ref,
    near_ref,
    far_ref,
    size_ref,
    own_ref,
    inner_v,
    sem,
):
    count = rows * slots
    outs = rows * quarter
    size = 2 * UNROLL
    load_a = pltpu.make_async_copy(blocks_ref, a_ref.at[pl.ds(0, count)], sem.at[1])
    load_a.start()
    load = pltpu.make_async_copy(inner_ref, inner_v.at[pl.ds(count, count)], sem.at[0])
    load.start()
    move_own = pltpu.make_async_copy(
        a_ref.at[pl.ds(0, count)], inner_v.at[pl.ds(0, count)], sem.at[2]
    )
    a_ref[count] = jnp.zeros(a_ref.shape[1:], a_ref.dtype)

    def clear(o, carry):
        acc_ref[o] = jnp.zeros(acc_ref.shape[1:], acc_ref.dtype)
        return carry

    lax.fori_loop(0, outs + 1, clear, 0)
    start_slot = start_ref[0]

    def one_row(i, ends):
        base = i * slots
        row_tag = base << 10
        terms_at = [place_ref[base + m] * (STRIDE - 1) for m in range(slots)]

        def one_output(p, ends):
            j_at = place_ref[base + start_slot + p]
            tag = row_tag + ((i * quarter + p) << 18)

            def terms(ends):
                e_own, e_near, e_far = ends
                for m in range(slots):
                    code = table_ref[terms_at[m] + (j_at + 2 * BAND)]
                    entry = code + (tag + (m << 10))
                    own_ref[e_own] = entry
                    near_ref[e_near] = entry
                    far_ref[e_far] = entry
                    e_own += (code >> 25) & 1
                    e_near += (code >> 26) & 1
                    e_far += code >> 27
                none = ((i * quarter + p) << 18) | (count << 10)
                own_ref[e_own] = none
                near_ref[e_near] = none
                far_ref[e_far] = none
                return e_own + (e_own & 1), e_near + (e_near & 1), e_far + (e_far & 1)

            return lax.cond(j_at < 3 * rows, terms, lambda ends: ends, ends)

        return lax.fori_loop(0, quarter, one_output, ends)

    zero = jnp.int32(0)
    half = lax.fori_loop(0, rows // 2, one_row, (zero, zero, zero))
    load_a.wait()
    move_own.start()
    e_own, e_near, e_far = lax.fori_loop(rows // 2, rows, one_row, half)
    for u in range(size):
        none = (outs << 18) | (count << 10)
        own_ref[e_own + u] = none
        near_ref[e_near + u] = none
        far_ref[e_far + u] = none
    size_ref[0] = (e_near + size - 1) // size * size
    size_ref[1] = (e_far + size - 1) // size * size
    move_own.wait()
    load.wait()
    run_list(own_ref, (e_own + size - 1) // size * size, a_ref, inner_v, acc_ref)


def local_products(start, table, place, blocks, inner, rows, slots, quarter):
    edge = blocks.shape[-1]
    outs = rows * quarter
    length = outs * slots + 4 * UNROLL
    return pl.pallas_call(
        functools.partial(local_kernel, rows, slots, quarter),
        out_shape=(
            jax.ShapeDtypeStruct((outs + 1, edge, edge), jnp.float32),
            jax.ShapeDtypeStruct((rows * slots + 1, edge, edge), blocks.dtype),
            jax.ShapeDtypeStruct((length,), jnp.int32),
            jax.ShapeDtypeStruct((length,), jnp.int32),
            jax.ShapeDtypeStruct((8,), jnp.int32),
        ),
        in_specs=[SMEM, SMEM, SMEM, ANY, ANY],
        out_specs=(VMEM, VMEM, SMEM, SMEM, SMEM),
        scratch_shapes=[
            pltpu.SMEM((length,), jnp.int32),
            pltpu.VMEM((2 * rows * slots, edge, edge), blocks.dtype),
            pltpu.SemaphoreType.DMA((3,)),
        ],
        compiler_params=pltpu.CompilerParams(vmem_limit_bytes=32 << 20),
        cost_estimate=pl.CostEstimate(
            flops=2 * 10**9, bytes_accessed=8 * 10**6, transcendentals=0
        ),
        name="local_products",
    )(start, table, place, blocks, inner)


def near_kernel(
    layer_ref,
    size_ref,
    list_ref,
    acc_in,
    a_ref,
    near0_ref,
    near1_ref,
    near2_ref,
    near3_ref,
    acc_ref,
    v_ref,
    sem,
):
    nears = (near0_ref, near1_ref, near2_ref, near3_ref)
    near = near0_ref.shape[0]
    copies = []
    for away, ref in enumerate(nears):
        source = lax.rem(layer_ref[0] + len(nears) - away, len(nears))
        copies.append(
            pltpu.make_async_copy(
                ref, v_ref.at[pl.ds(source * near, near)], sem.at[away]
            )
        )
    for copy in copies:
        copy.start()
    for copy in copies:
        copy.wait()
    run_list(list_ref, size_ref[0], a_ref, v_ref, acc_ref)


def near_products(layer, size, entries, acc, blocks, nears):
    edge = blocks.shape[-1]
    held = len(nears) * nears[0].shape[0]
    return pl.pallas_call(
        near_kernel,
        out_shape=jax.ShapeDtypeStruct(acc.shape, acc.dtype),
        in_specs=[SMEM] * 3 + [VMEM, VMEM] + [ANY] * len(nears),
        out_specs=VMEM,
        scratch_shapes=[
            pltpu.VMEM((held, edge, edge), blocks.dtype),
            pltpu.SemaphoreType.DMA((len(nears),)),
        ],
        input_output_aliases={3: 0},
        compiler_params=pltpu.CompilerParams(vmem_limit_bytes=24 << 20),
        name="near_products",
    )(layer, size, entries, acc, blocks, *nears)


def far_kernel(
    rows,
    quarter,
    more_ref,
    size_ref,
    list_ref,
    acc_in,
    a_ref,
    first_ref,
    late_ref,
    out_ref,
    acc_ref,
    v_ref,
    held,
    sem,
):
    first, late = first_ref.shape[0], late_ref.shape[0]

    @pl.when(more_ref[0] == 0)
    def _():
        run_list(list_ref, size_ref[1], a_ref, first_ref, acc_ref)

    @pl.when(more_ref[0] != 0)
    def _():
        late_copy = pltpu.make_async_copy(
            late_ref, v_ref.at[pl.ds(first, late)], sem.at[0]
        )
        late_copy.start()

        def move(b, carry):
            v_ref[b] = first_ref[b]
            return carry

        lax.fori_loop(0, first, move, 0)
        late_copy.wait()
        run_list(list_ref, size_ref[1], a_ref, v_ref, acc_ref)

    def finish(i, carry):
        part = pl.ds(i * quarter, quarter)
        held[part] = acc_ref[part].astype(held.dtype)
        pltpu.make_async_copy(held.at[part], out_ref.at[part], sem.at[1]).start()
        return carry

    lax.fori_loop(0, rows, finish, 0)
    pltpu.make_async_copy(held, out_ref, sem.at[1]).wait()


def far_products(more, size, entries, acc, blocks, first, late, rows, quarter):
    edge = blocks.shape[-1]
    outs = rows * quarter
    held = first.shape[0] + late.shape[0]
    square, _ = pl.pallas_call(
        functools.partial(far_kernel, rows, quarter),
        out_shape=(
            jax.ShapeDtypeStruct((outs, edge, edge), blocks.dtype),
            jax.ShapeDtypeStruct(acc.shape, acc.dtype),
        ),
        in_specs=[SMEM] * 3 + [VMEM, VMEM, VMEM, ANY],
        out_specs=(ANY, VMEM),
        scratch_shapes=[
            pltpu.VMEM((held, edge, edge), blocks.dtype),
            pltpu.VMEM((outs, edge, edge), blocks.dtype),
            pltpu.SemaphoreType.DMA((2,)),
        ],
        input_output_aliases={3: 1},
        compiler_params=pltpu.CompilerParams(vmem_limit_bytes=24 << 20),
        name="far_products",
    )(more, size, entries, acc, blocks, first, late)
    return square


def blank(shape, dtype):
    return pl.pallas_call(
        lambda out_ref: None,
        out_shape=jax.ShapeDtypeStruct(shape, dtype),
        out_specs=ANY,
        name="blank",
    )()


def or_reduce(x, axis):
    return lax.reduce(x, jnp.uint32(0), lax.bitwise_or, (axis,))


def bit_masks(off, live):
    bits = jnp.where(live, jnp.uint32(1) << off.astype(jnp.uint32), jnp.uint32(0))
    return or_reduce(bits, 1), bits


def needed(k_mask, i_mask, i_part, later):
    rows = k_mask.shape[-1]
    kk = lax.broadcasted_iota(jnp.int32, (rows, rows), 0)
    ii = lax.broadcasted_iota(jnp.int32, (rows, rows), 1)
    ahead = ii - kk if later else kk - ii
    valid = ahead <= 0
    shift = jnp.where(valid, rows + ahead, 0).astype(jnp.uint32)
    at = BAND - shift if later else BAND + shift
    has = valid & (((i_mask[..., None, :] >> at) & 1) == 1)
    moved = i_part[..., None, :] << shift if later else i_part[..., None, :] >> shift
    return k_mask & or_reduce(jnp.where(has, moved, jnp.uint32(0)), moved.ndim - 1)


def most_needed(columns, counts, layers):
    total_rows, slots = columns.shape
    quarter = slots // layers
    rows_id = jnp.arange(total_rows, dtype=jnp.int32)
    off = (columns - rows_id[:, None] + BAND) % total_rows
    slot_ids = jnp.arange(slots, dtype=jnp.int32)
    live = slot_ids[None, :] < counts[:, None]
    mask, bits = bit_masks(off, live)
    part = jnp.stack(
        [or_reduce(bits[:, q * quarter : (q + 1) * quarter], 1) for q in range(layers)]
    )
    mask_wrap = jnp.concatenate([mask[-BAND:], mask, mask[:BAND]])
    part_wrap = jnp.concatenate([part[:, -BAND:], part, part[:, :BAND]], axis=1)
    kk = rows_id % BAND
    up = jnp.zeros_like(part)
    down = jnp.zeros_like(part)
    for s in range(1, BAND + 1):
        i_mask = mask_wrap[BAND + s : BAND + s + total_rows]
        i_part = part_wrap[:, BAND + s : BAND + s + total_rows]
        has = (((i_mask >> (BAND - s)) & 1) == 1) & (kk + s >= BAND)
        up = up | jnp.where(has, i_part << s, jnp.uint32(0))
        i_mask = mask_wrap[BAND - s : BAND - s + total_rows]
        i_part = part_wrap[:, BAND - s : BAND - s + total_rows]
        has = (((i_mask >> (BAND + s)) & 1) == 1) & (kk - s < 0)
        down = down | jnp.where(has, i_part >> s, jnp.uint32(0))
    odd = (rows_id // BAND) % 2 == 1
    fixed = or_reduce(bits[:, :NEAR_SLOTS], 1)
    close = jnp.where(odd, kk >= BAND - NEAR_ROWS, kk < NEAR_ROWS)
    asked = jnp.where(odd, up, down) & mask & jnp.where(close, ~fixed, ~jnp.uint32(0))
    per_row = lax.population_count(asked).astype(jnp.bfloat16)
    member = np.arange(total_rows)[:, None] // BAND == np.arange(total_rows // BAND)
    per_group = jnp.dot(
        per_row, jnp.asarray(member, jnp.bfloat16), preferred_element_type=jnp.float32
    )
    return jnp.max(per_group)


def per_device(values, columns, counts):
    rows, slots, edge, _ = values.shape
    layers = lax.axis_size("layer")
    quarter = slots // layers
    start_slot = lax.axis_index("layer") * quarter
    total_rows = columns.shape[0]
    group = lax.axis_index(("row", "col"))
    groups = lax.axis_size(("row", "col"))
    even = group % 2 == 0
    first_row = group * rows
    blocks = values.reshape((-1, edge, edge))
    span = rows * slots

    inner = lax.ppermute(blocks, ("row", "col"), [(g, g ^ 1) for g in range(groups)])

    share = NEAR_SLOTS // layers
    layer = lax.axis_index("layer")
    outer_pairs = [
        (g, (g - 1) % groups if g % 2 == 0 else (g + 1) % groups) for g in range(groups)
    ]
    near_rows = lax.dynamic_slice(
        values,
        (jnp.where(even, 0, rows - NEAR_ROWS), layer * share, 0, 0),
        (NEAR_ROWS, share, edge, edge),
    ).reshape(-1, edge, edge)
    near_mine = lax.ppermute(near_rows, ("row", "col"), outer_pairs)
    both = jnp.concatenate([columns.T, counts[None, :]], axis=0)
    both = lax.optimization_barrier(both)
    both = jnp.concatenate([both[:, -rows:], both, both[:, :rows]], axis=1)
    both = lax.dynamic_slice_in_dim(both, first_row, 3 * rows, 1)
    cols, cnts = both[:slots].T, both[slots]
    row_ids = first_row - rows + jnp.arange(3 * rows, dtype=jnp.int32)
    off = (cols - row_ids[:, None] + BAND) % total_rows
    slot_ids = jnp.arange(slots, dtype=jnp.int32)[None, :]
    live = slot_ids < cnts[:, None]
    mask, bits = bit_masks(off, live)
    mine = (slot_ids >= start_slot) & (slot_ids < start_slot + quarter)
    part = or_reduce(jnp.where(mine, bits, jnp.uint32(0)), 1)
    mask = mask.reshape(3, rows)
    part = part.reshape(3, rows)
    off = off.reshape(3, rows, slots)
    live = live.reshape(3, rows, slots)

    def pair(x):
        return jnp.where(even, x[:2], x[1:])

    mask2, part2, off2, live2 = pair(mask), pair(part), pair(off), pair(live)
    ask = jnp.stack(
        [
            needed(mask2[0], mask2[1], part2[1], True),
            needed(mask2[1], mask2[0], part2[0], False),
        ]
    )
    need = (((ask[:, :, None] >> off2.astype(jnp.uint32)) & 1) == 1) & live2
    fixed = (jnp.arange(rows)[:, None] < NEAR_ROWS) & (slot_ids < NEAR_SLOTS)
    need = jnp.stack([need[0, ::-1], need[1]]) & ~fixed
    need = need.reshape(2, span)
    before = (
        lax.broadcasted_iota(jnp.int32, (span, span), 0)
        < lax.broadcasted_iota(jnp.int32, (span, span), 1)
    ).astype(jnp.bfloat16)
    pos = jnp.dot(
        need.astype(jnp.bfloat16), before, preferred_element_type=jnp.float32
    ).astype(jnp.int32)
    ids = jnp.arange(span, dtype=jnp.int32)
    ids_up = (rows - 1 - ids // slots) * slots + ids % slots
    give, give_pos = jnp.where(even, need[1], need[0]), jnp.where(even, pos[1], pos[0])
    give_ids = jnp.where(even, ids, ids_up)
    get, get_pos = jnp.where(even, need[0], need[1]), jnp.where(even, pos[0], pos[1])
    hit = give[:, None] & (
        give_pos[:, None] == jnp.arange(BOUND, dtype=jnp.int32)[None, :]
    )
    send_idx = jnp.sum(jnp.where(hit, give_ids[:, None], 0), axis=0)

    packed = pack(send_idx, blocks, 0, FIRST)
    _, near_mine, columns, counts = lax.optimization_barrier(
        (packed, near_mine, columns, counts)
    )
    nears = [near_mine] + [
        lax.ppermute(near_mine, "layer", [(x, (x + d) % layers) for x in range(layers)])
        for d in range(1, layers)
    ]
    outer = lax.ppermute(packed, ("row", "col"), outer_pairs)

    code = jnp.where(get, (4 << 25) + get_pos, 0)
    code = jnp.where(even, code.reshape(rows, slots)[::-1], code.reshape(rows, slots))
    row_at = jnp.arange(rows, dtype=jnp.int32)[:, None] - jnp.where(even, rows - NEAR_ROWS, 0)
    sent = (row_at >= 0) & (row_at < NEAR_ROWS) & (slot_ids < NEAR_SLOTS)
    sent_at = (slot_ids // share * NEAR_ROWS + row_at) * share + slot_ids % share
    far_live = jnp.where(even, live[0], live[2])
    code = jnp.where(sent & far_live, (2 << 25) + sent_at, code)
    ids = ids.reshape(rows, slots)
    own = jnp.where(live[1], (1 << 25) + ids, 0)
    near = jnp.where(even, live[2], live[0])
    near = jnp.where(near, (1 << 25) + span + ids, 0)
    codes = jnp.concatenate(
        [jnp.where(even, code, near), own, jnp.where(even, near, code)], axis=0
    )
    off3 = off.reshape(3 * rows, slots)
    at = lax.broadcasted_iota(jnp.int32, (1, 1, STRIDE), 2)
    table = jnp.sum(
        jnp.where(off3[:, :, None] + BAND == at, codes[:, :, None], 0), axis=1
    ).reshape(-1)
    table = jnp.concatenate([table, jnp.zeros((STRIDE,), jnp.int32)])
    place = jnp.where(
        live[1], jnp.arange(rows, dtype=jnp.int32)[:, None] + off[1], 3 * rows
    ).reshape(-1)
    inner, columns, counts = lax.optimization_barrier((inner, columns, counts))
    more = most_needed(columns, counts, layers) > FIRST

    def second():
        late = pack(send_idx, blocks, FIRST, BOUND - FIRST)
        return lax.ppermute(late, ("row", "col"), outer_pairs)

    late = lax.cond(
        more, second, lambda: blank((BOUND - FIRST, edge, edge), values.dtype)
    )
    start = jnp.full((8,), start_slot, jnp.int32)

    acc, held, near_list, far_list, size = local_products(
        start, table, place, blocks, inner, rows, slots, quarter
    )
    acc = near_products(jnp.full((8,), layer, jnp.int32), size, near_list, acc, held, nears)
    more = jnp.full((8,), more, jnp.int32)
    square = far_products(more, size, far_list, acc, held, outer, late, rows, quarter)
    return square.reshape(rows, quarter, edge, edge)


def solution(mesh):
    return jax.shard_map(
        per_device,
        mesh=mesh,
        in_specs=(P(("row", "col"), None, None, None), P(), P()),
        out_specs=P(("row", "col"), "layer", None, None),
        check_vma=False,
    )
```
